32 devices in a mesh: inline: 2 (over x), xline: 16 (over z, y, core).
Axes of the slice: x: 2, y: 2, z: 4, core: 2. Of those that a mesh axis runs over, the one named last changes fastest.
Arguments:
- traces: float32 [16, 256, 1024], P('inline', 'xline'), may hold values from -6 to 6
- filters: float32 [2, 512, 81], replicated, may hold values from -0.6 to 0.6
Outputs:
- denoised: float32 [16, 256, 1024], P('inline', 'xline')
The draws below stay inside these ranges and needn't reach their ends.
All inputs are finite; a program needn't handle non-finite values.
Results may differ from the reference program's by a relative error of at most 0.00007.
Values sent between devices are 32-bit elements; how exact they have to be, the bound alone decides.
A program may use at most 64 MiB of HBM per device.

```python
import jax
import jax.numpy as jnp
from jax import lax

NT = 1024
NF = 512
NIL = 16
NXL = 256


def level_of(key, shape, split, smallest, largest):
    loudness, own = 1.0, jax.random.fold_in(key, 6)
    for position, shards_of in split:
        heights = jnp.exp(jax.random.uniform(jax.random.fold_in(own, position), (shards_of,), jnp.float32, smallest / len(split), largest / len(split)))
        loudness = loudness * jnp.repeat(heights, shape[position] // shards_of).reshape([-1 if axis == position else 1 for axis in range(len(shape))])
    return loudness


def gaussian(key, shape, spread, most, pieces=(), kind=jnp.bfloat16):
    gain = level_of(key, shape, pieces, -0.22, 0.18) if pieces else 1.0
    values = jax.random.normal(key, shape, jnp.float32) * spread * gain
    return jnp.minimum(jnp.maximum(values, -most), most).astype(kind)


def setup_inputs(seed: int = 0) -> dict:
    key_list = jax.random.split(jax.random.key(seed), 3)
    return {
        "traces": gaussian(key_list[0], (NIL, NXL, NT), 1.0, 6.0, ((0, 2), (1, 16)), jnp.float32),
        "filters": gaussian(key_list[1], (2, NF, 81), 0.1, 0.6, (), jnp.float32),
    }


def filter_bin(operands):
    plane_real, plane_imag, taps_real, taps_imag = operands
    rows_total = plane_real.shape[0]
    cols_total = plane_real.shape[1]
    padded_real = jnp.pad(plane_real, 4)
    padded_imag = jnp.pad(plane_imag, 4)
    total_real = jnp.zeros_like(plane_real)
    total_imag = jnp.zeros_like(plane_imag)
    for shift_row in range(9):
        for shift_col in range(9):
            index_tap = shift_row * 9 + shift_col
            piece_real = padded_real[shift_row:shift_row + rows_total, shift_col:shift_col + cols_total]
            piece_imag = padded_imag[shift_row:shift_row + rows_total, shift_col:shift_col + cols_total]
            total_real = total_real + taps_real[index_tap] * piece_real - taps_imag[index_tap] * piece_imag
            total_imag = total_imag + taps_real[index_tap] * piece_imag + taps_imag[index_tap] * piece_real
    return total_real, total_imag


def reference(traces, filters):
    spectrum = jnp.fft.rfft(traces, axis=-1)[:, :, :NF]
    spec_real = jnp.transpose(jnp.real(spectrum), (2, 0, 1))
    spec_imag = jnp.transpose(jnp.imag(spectrum), (2, 0, 1))
    out_real, out_imag = lax.map(filter_bin, (spec_real, spec_imag, filters[0], filters[1]))
    filtered = jnp.transpose(out_real, (1, 2, 0)) + 1j * jnp.transpose(out_imag, (1, 2, 0))
    full_bins = jnp.pad(filtered, ((0, 0), (0, 0), (0, NT // 2 + 1 - NF)))
    denoised = jnp.fft.irfft(full_bins, n=NT, axis=-1)
    return denoised.astype(jnp.float32)
```

```python
import functools

import jax
import jax.numpy as jnp
import ml_dtypes
import numpy as np
from jax import lax
from jax.experimental import pallas as pl
from jax.experimental.pallas import tpu as pltpu
from jax.sharding import PartitionSpec as P

HALF = 4
TAPS = 9
MESH = pl.DeviceIdType.MESH
BF16 = jnp.bfloat16
F32 = jnp.float32


def halves(table):
    high = table.astype(np.float32).astype(ml_dtypes.bfloat16)
    low = (table - high.astype(np.float64)).astype(np.float32).astype(ml_dtypes.bfloat16)
    return np.stack((high, low))


def temporal_tables(samples, frequencies):
    fold = samples // 2
    time = np.arange(fold)[:, None]
    forward, inverse = [], []
    for parity in range(2):
        bins = np.arange(parity, frequencies, 2)[None, :]
        angle = 2.0 * np.pi * (time * bins % samples) / samples
        weight = np.where(bins == 0, 1.0, 2.0) / samples
        forward.append(np.concatenate((np.cos(angle), -np.sin(angle)), axis=1))
        inverse.append(np.concatenate((weight * np.cos(angle), -weight * np.sin(angle)), axis=1).T)
    return halves(np.stack(forward)), halves(np.stack(inverse))


def spatial_frequencies(height, width):
    chosen = []
    for row in range(height):
        for col in range(width):
            mirror = ((height - row) % height, (width - col) % width)
            if (row, col) <= mirror:
                chosen.append((row, col, 1.0 if (row, col) == mirror else 2.0))
    return np.array(chosen)


def spatial_basis(waves, padded, height, width, positions):
    positions = np.asarray(positions)
    turns = np.outer(waves[:, 0], positions[:, 0]) / height + np.outer(waves[:, 1], positions[:, 1]) / width
    angle = 2.0 * np.pi * turns
    basis = np.zeros((2 * padded, len(positions)))
    basis[: len(waves)] = np.cos(angle)
    basis[padded : padded + len(waves)] = np.sin(angle)
    return basis


def grid(rows, cols):
    return [(row, col) for row in rows for col in cols]


def spatial_tables(rows, cols, inline_count):
    height, width = rows + 2 * HALF, cols + 2 * HALF
    waves = spatial_frequencies(height, width)
    padded = -(-len(waves) // 16) * 16
    basis = functools.partial(spatial_basis, waves, padded, height, width)
    low, high = range(-HALF, 0), range(cols, cols + HALF)
    own = grid(range(rows), range(cols))
    first = basis(own + grid(range(rows), low) + grid(range(rows), high))
    above, below = range(-HALF, 0), range(rows, rows + HALF)
    if inline_count == 2:
        variants = [[below], [above]]
    else:
        variants = [[above, below]]
    second = []
    for sides in variants:
        places = []
        for side in sides:
            places += grid(side, range(cols))
        for side in sides:
            places += grid(side, low) + grid(side, high)
        second.append(halves(basis(places)))
    taps = basis(grid(range(-HALF, HALF + 1), range(-HALF, HALF + 1)))
    count = np.zeros((2 * padded, 1))
    count[: len(waves), 0] = waves[:, 2] / (height * width)
    count[padded : padded + len(waves), 0] = -waves[:, 2] / (height * width)
    back = (count * basis(own)).T
    return halves(first), np.stack(second), halves(taps), halves(back)


def parts(value):
    high = value.astype(BF16)
    return high, (value - high.astype(F32)).astype(BF16)


def product(left, right, dims=(((1,), (0,)), ((), ()))):
    dot = functools.partial(lax.dot_general, dimension_numbers=dims, preferred_element_type=F32)
    return dot(left[0], right[0]) + (dot(left[0], right[1]) + dot(left[1], right[0]))


def kernel(
    rows, cols, inline_count, xline_count,
    traces, filters, forward, inverse, first, second, taps, back,
    out,
    place, spec_high, spec_low, edge, corner, kept, wave, response,
    taps_in, forward_in, inverse_in, first_in, second_in, tapm_in, back_in,
    local_sem, send_sem, recv_sem,
):
    sides = min(inline_count - 1, 2)
    own = rows * cols
    strip = rows * HALF
    band = HALF * cols
    spot = HALF * HALF
    samples = place.shape[1]
    fold = samples // 2
    quarter = fold // 2
    padded = wave.shape[0] // 2
    left_at, right_at = own, own + strip
    band_at = own + 2 * strip
    spot_at = band_at + sides * band
    total = spot_at + sides * 2 * spot

    me_i = lax.axis_index("inline")
    me_x = lax.axis_index("xline")

    loads = [
        pltpu.make_async_copy(traces, place.at[pl.ds(0, own)], local_sem.at[0]),
        pltpu.make_async_copy(forward, forward_in, local_sem.at[1]),
        pltpu.make_async_copy(filters, taps_in, local_sem.at[2]),
        pltpu.make_async_copy(taps, tapm_in, local_sem.at[3]),
        pltpu.make_async_copy(first, first_in, local_sem.at[4]),
        pltpu.make_async_copy(second.at[me_i if inline_count == 2 else 0], second_in, local_sem.at[5]),
        pltpu.make_async_copy(back, back_in, local_sem.at[6]),
        pltpu.make_async_copy(inverse, inverse_in, local_sem.at[7]),
    ]
    for load in loads:
        load.start()

    has_left, has_right = me_x > 0, me_x < xline_count - 1
    neighbours = [(has_left, {"xline": me_x - 1}), (has_right, {"xline": me_x + 1})]
    if inline_count == 2:
        bands = [(None, {"inline": 1 - me_i}, (1 - me_i) * ((rows - HALF) * cols), 0)]
    elif inline_count > 2:
        bands = [
            (me_i > 0, {"inline": me_i - 1}, 0, 1),
            (me_i < inline_count - 1, {"inline": me_i + 1}, (rows - HALF) * cols, 0),
        ]
    else:
        bands = []
    neighbours += [(exists, where) for exists, where, _, _ in bands]

    def when(condition, action):
        if condition is None:
            action()
        else:
            pl.when(condition)(action)

    barrier = pltpu.get_barrier_semaphore()
    for exists, where in neighbours:
        when(exists, lambda: pl.semaphore_signal(barrier, inc=1, device_id=where, device_id_type=MESH))
    peers = sum(1 if exists is None else exists.astype(jnp.int32) for exists, _ in neighbours)
    pl.semaphore_wait(barrier, peers)

    def remote(source, target_at, size, slot, where):
        return pltpu.make_async_remote_copy(
            src_ref=source,
            dst_ref=place.at[pl.ds(target_at, size)],
            send_sem=send_sem.at[slot],
            recv_sem=recv_sem.at[slot],
            device_id=where,
            device_id_type=MESH,
        )

    for exists, where, start, lands in bands:
        start = pl.multiple_of(start, 8)
        copy = remote(traces.at[pl.ds(start, band)], band_at + lands * band, band, 2 + lands, where)
        when(exists, copy.start)

    loads[0].wait()
    for row in range(rows):
        at = row * cols
        edge[0, row * HALF : (row + 1) * HALF, :] = place[at : at + HALF, :]
        edge[1, row * HALF : (row + 1) * HALF, :] = place[at + cols - HALF : at + cols, :]
    to_left = remote(edge.at[0], right_at, strip, 1, {"xline": me_x - 1})
    to_right = remote(edge.at[1], left_at, strip, 0, {"xline": me_x + 1})
    when(has_left, to_left.start)
    when(has_right, to_right.start)

    loads[2].wait()
    loads[3].wait()
    across = (((1,), (1,)), ((), ()))
    for parity in range(2):
        for part in range(2):
            lanes = slice((2 * parity + part) * quarter, (2 * parity + part + 1) * quarter)
            coefficients = taps_in[part, pl.ds(parity, quarter, stride=2), :]
            response[:, lanes] = product((tapm_in[0], tapm_in[1]), parts(coefficients), across)

    def spectra(start, size):
        block = place[start : start + size, :]
        folded = (block[:, :fold] + block[:, fold:], block[:, :fold] - block[:, fold:])
        for parity in range(2):
            lanes = slice(parity * fold, (parity + 1) * fold)
            spectrum = product(parts(folded[parity]), (forward_in[0, parity], forward_in[1, parity]))
            high, low = parts(spectrum)
            spec_high[start : start + size, lanes] = high
            spec_low[start : start + size, lanes] = low

    loads[1].wait()
    spectra(0, own)

    for exists, copy, at in ((has_left, to_right, left_at), (has_right, to_left, right_at)):
        when(exists, copy.wait_recv)

        def clear(at=at):
            place[at : at + strip, :] = jnp.zeros((strip, samples), F32)

        pl.when(jnp.logical_not(exists))(clear)
    spectra(own, 2 * strip)
    loads[4].wait()
    for parity in range(2):
        lanes = slice(parity * fold, (parity + 1) * fold)
        wave[:, lanes] = product(
            (first_in[0], first_in[1]), (spec_high[:band_at, lanes], spec_low[:band_at, lanes])
        )

    for lands in range(sides):
        at = band_at + lands * band
        if inline_count == 2:
            exists = None
        else:
            exists = (me_i > 0) if lands == 0 else (me_i < inline_count - 1)
        incoming = remote(traces.at[pl.ds(0, band)], at, band, 2 + lands, {"xline": me_x})
        spots = [spot_at + (2 * lands + side) * spot for side in range(2)]
        slots = [4 + 2 * lands + side for side in range(2)]
        go_right = remote(corner.at[lands, 1], spots[0], spot, slots[0], {"xline": me_x + 1})
        go_left = remote(corner.at[lands, 0], spots[1], spot, slots[1], {"xline": me_x - 1})

        def arrive():
            incoming.wait_recv()
            for row in range(HALF):
                here = at + row * cols
                corner[lands, 0, row * HALF : (row + 1) * HALF, :] = place[here : here + HALF, :]
                corner[lands, 1, row * HALF : (row + 1) * HALF, :] = place[here + cols - HALF : here + cols, :]
            pl.when(has_right)(go_right.start)
            pl.when(has_left)(go_left.start)

        def absent():
            place[at : at + band, :] = jnp.zeros((band, samples), F32)
            for side in range(2):
                place[spots[side] : spots[side] + spot, :] = jnp.zeros((spot, samples), F32)

        when(exists, arrive)
        if exists is not None:
            pl.when(jnp.logical_not(exists))(absent)
    if sides:
        spectra(band_at, sides * band)
    for lands in range(sides):
        if inline_count == 2:
            exists = None
        else:
            exists = (me_i > 0) if lands == 0 else (me_i < inline_count - 1)
        for side, has in ((0, has_left), (1, has_right)):
            at = spot_at + (2 * lands + side) * spot
            come = remote(corner.at[lands, side], at, spot, 4 + 2 * lands + side, {"xline": me_x})

            def clear(at=at):
                place[at : at + spot, :] = jnp.zeros((spot, samples), F32)

            def get():
                pl.when(has)(come.wait_recv)
                pl.when(jnp.logical_not(has))(clear)

            when(exists, get)
    if sides:
        spectra(spot_at, sides * 2 * spot)
        loads[5].wait()
        for parity in range(2):
            lanes = slice(parity * fold, (parity + 1) * fold)
            wave[:, lanes] += product(
                (second_in[0], second_in[1]), (spec_high[band_at:total, lanes], spec_low[band_at:total, lanes])
            )
    else:
        loads[5].wait()

    loads[6].wait()
    loads[7].wait()
    halfway = []
    for parity in range(2):
        real = slice(2 * parity * quarter, (2 * parity + 1) * quarter)
        imag = slice((2 * parity + 1) * quarter, (2 * parity + 2) * quarter)
        rc, rs = wave[:padded, real], wave[padded:, real]
        ic, js = wave[:padded, imag], wave[padded:, imag]
        frc, frs = response[:padded, real], response[padded:, real]
        fic, fis = response[:padded, imag], response[padded:, imag]
        outcome = {
            (0, 0): rc * frc + rs * frs - (ic * fic + js * fis),
            (1, 0): rc * frs - rs * frc - (ic * fis - js * fic),
            (0, 1): rc * fic + rs * fis + (ic * frc + js * frs),
            (1, 1): rc * fis - rs * fic + (ic * frs - js * frc),
        }
        for (which, part), value in outcome.items():
            high, low = parts(value)
            kept[0, which * padded : (which + 1) * padded, part * quarter : (part + 1) * quarter] = high
            kept[1, which * padded : (which + 1) * padded, part * quarter : (part + 1) * quarter] = low
        filtered = product((back_in[0], back_in[1]), (kept[0], kept[1]))
        halfway.append(product(parts(filtered), (inverse_in[0, parity], inverse_in[1, parity])))
    out[:, :fold] = halfway[0] + halfway[1]
    out[:, fold:] = halfway[0] - halfway[1]

    when(has_left, to_left.wait_send)
    when(has_right, to_right.wait_send)
    for exists, where, start, lands in bands:
        copy = remote(traces.at[pl.ds(pl.multiple_of(start, 8), band)], band_at + lands * band, band, 2 + lands, where)
        when(exists, copy.wait_send)
    for lands in range(sides):
        if inline_count == 2:
            exists = None
        else:
            exists = (me_i > 0) if lands == 0 else (me_i < inline_count - 1)
        spots = [spot_at + (2 * lands + side) * spot for side in range(2)]
        go_right = remote(corner.at[lands, 1], spots[0], spot, 4 + 2 * lands, {"xline": me_x + 1})
        go_left = remote(corner.at[lands, 0], spots[1], spot, 5 + 2 * lands, {"xline": me_x - 1})

        def sent():
            pl.when(has_right)(go_right.wait_send)
            pl.when(has_left)(go_left.wait_send)

        when(exists, sent)


def per_device(traces, filters, inline_count, xline_count):
    rows, cols, samples = traces.shape
    frequencies = filters.shape[1]
    forward, inverse = temporal_tables(samples, frequencies)
    first, second, taps, back = spatial_tables(rows, cols, inline_count)
    sides = min(inline_count - 1, 2)
    own = rows * cols
    total = own + 2 * rows * HALF + sides * (HALF * cols + 2 * HALF * HALF)
    waves = first.shape[1]
    operands = [traces.reshape(own, samples), filters] + [
        jnp.asarray(table) for table in (forward, inverse, first, second, taps, back)
    ]
    result = pl.pallas_call(
        functools.partial(kernel, rows, cols, inline_count, xline_count),
        out_shape=jax.ShapeDtypeStruct((own, samples), F32),
        in_specs=[pl.BlockSpec(memory_space=pl.ANY)] * len(operands),
        out_specs=pl.BlockSpec(memory_space=pltpu.VMEM),
        scratch_shapes=[
            pltpu.VMEM((total, samples), F32),
            pltpu.VMEM((total, samples), BF16),
            pltpu.VMEM((total, samples), BF16),
            pltpu.VMEM((2, rows * HALF, samples), F32),
            pltpu.VMEM((max(sides, 1), 2, HALF * HALF, samples), F32),
            pltpu.VMEM((2, waves, samples // 2), BF16),
            pltpu.VMEM((waves, samples), F32),
            pltpu.VMEM((waves, samples), F32),
            pltpu.VMEM(filters.shape, F32),
            pltpu.VMEM(forward.shape, BF16),
            pltpu.VMEM(inverse.shape, BF16),
            pltpu.VMEM(first.shape, BF16),
            pltpu.VMEM(second.shape[1:], BF16),
            pltpu.VMEM(taps.shape, BF16),
            pltpu.VMEM(back.shape, BF16),
            pltpu.SemaphoreType.DMA((8,)),
            pltpu.SemaphoreType.DMA((8,)),
            pltpu.SemaphoreType.DMA((8,)),
        ],
        compiler_params=pltpu.CompilerParams(
            collective_id=0, has_side_effects=True, vmem_limit_bytes=48 * 1024 * 1024
        ),
    )(*operands)
    return result.reshape(rows, cols, samples)


def solution(mesh):
    return jax.shard_map(
        functools.partial(
            per_device, inline_count=mesh.shape["inline"], xline_count=mesh.shape["xline"]
        ),
        mesh=mesh,
        in_specs=(P("inline", "xline", None), P()),
        out_specs=P("inline", "xline", None),
        check_vma=False,
    )
```

```python
import functools

import jax
import jax.numpy as jnp
import ml_dtypes
import numpy as np
from jax import lax
from jax.experimental import pallas as pl
from jax.experimental.pallas import tpu as pltpu
from jax.sharding import PartitionSpec as P

HALF = 4
GROUPS = 2
TAP_ROWS = 96
MESH = pl.DeviceIdType.MESH
BF16 = jnp.bfloat16
F32 = jnp.float32


def halves(table):
    high = table.astype(np.float32).astype(ml_dtypes.bfloat16)
    low = (table - high.astype(np.float64)).astype(np.float32).astype(ml_dtypes.bfloat16)
    return np.stack((high, low))


def bin_groups(frequencies):
    order = np.concatenate((np.arange(0, frequencies, 2), np.arange(1, frequencies, 2)))
    return order.reshape(GROUPS, frequencies // GROUPS)


def temporal_tables(samples, frequencies):
    time = np.arange(samples // 2)[:, None]
    forward, inverse = [], []
    for bins in bin_groups(frequencies):
        angle = 2.0 * np.pi * (time * bins[None, :] % samples) / samples
        weight = np.where(bins == 0, 1.0, 2.0)[None, :] / samples
        forward.append(np.concatenate((np.cos(angle), -np.sin(angle)), axis=1))
        inverse.append(np.concatenate((weight * np.cos(angle), -weight * np.sin(angle)), axis=1).T)
    return halves(np.stack(forward)), halves(np.stack(inverse))


def spatial_frequencies(height, width):
    chosen = []
    for row in range(height):
        for col in range(width):
            mirror = ((height - row) % height, (width - col) % width)
            if (row, col) <= mirror:
                chosen.append((row, col, 1.0 if (row, col) == mirror else 2.0))
    return np.array(chosen)


def spatial_basis(waves, padded, height, width, positions):
    positions = np.asarray(positions)
    turns = np.outer(waves[:, 0], positions[:, 0]) / height + np.outer(waves[:, 1], positions[:, 1]) / width
    angle = 2.0 * np.pi * turns
    basis = np.zeros((2 * padded, len(positions)))
    basis[: len(waves)] = np.cos(angle)
    basis[padded : padded + len(waves)] = np.sin(angle)
    return basis


def grid(rows, cols):
    return [(row, col) for row in rows for col in cols]


def stacked(table):
    both = halves(table)
    return np.concatenate((both[0], both[1]), axis=0)


def layout(rows, cols, sides):
    strip, ends, middle = rows * HALF, HALF * HALF, HALF * (cols - 2 * HALF)
    sizes = [("left", strip), ("right", strip)]
    for side in range(sides):
        sizes += [(("low", side), ends), (("high", side), ends), (("middle", side), middle)]
        sizes += [(("from_left", side), ends), (("from_right", side), ends)]
    places, at = {}, 0
    for name, size in sizes:
        places[name] = (at, size)
        at += size
    return places, at


def spatial_tables(rows, cols, inline_count):
    height, width = rows + 2 * HALF, cols + 2 * HALF
    waves = spatial_frequencies(height, width)
    padded = -(-len(waves) // 16) * 16
    basis = functools.partial(spatial_basis, waves, padded, height, width)
    below_zero, above_end = range(-HALF, 0), range(cols, cols + HALF)
    own = grid(range(rows), range(cols))
    above, below = range(-HALF, 0), range(rows, rows + HALF)
    variants = [[below], [above]] if inline_count == 2 else [[above, below]]
    sides = min(inline_count - 1, 2)
    second = []
    for bands in variants:
        places = grid(range(rows), below_zero) + grid(range(rows), above_end)
        for band in bands[:sides]:
            places += grid(band, range(HALF)) + grid(band, range(cols - HALF, cols))
            places += grid(band, range(HALF, cols - HALF))
            places += grid(band, below_zero) + grid(band, above_end)
        second.append(stacked(basis(places)))
    reach = range(-HALF, HALF + 1)
    taps = np.zeros((2 * padded, TAP_ROWS))
    taps[:, : len(reach) ** 2] = basis(grid(reach, reach))
    count = np.zeros((2 * padded, 1))
    count[: len(waves), 0] = waves[:, 2] / (height * width)
    count[padded : padded + len(waves), 0] = -waves[:, 2] / (height * width)
    back = (count * basis(own)).T
    return stacked(basis(own)), np.stack(second), stacked(taps), stacked(back)


def parts(value):
    high = value.astype(BF16)
    return high, (value - high.astype(F32)).astype(BF16)


def product(left, high, low):
    dot = functools.partial(jnp.dot, preferred_element_type=F32)
    count = left.shape[0] // 2
    both = dot(left, high)
    return both[:count] + (both[count:] + dot(left[:count], low))


def kernel(
    rows, cols, inline_count, xline_count,
    traces, filters, forward, inverse, first, second, taps, back, order,
    out,
    own_in, own, own_high, own_low, ends, middle, halo, wave, response, kept, tap_rows,
    filters_in, forward_in, inverse_in, first_in, second_in, taps_in, back_in, order_in,
    local_sem, send_sem, recv_sem,
):
    sides = min(inline_count - 1, 2)
    places, _ = layout(rows, cols, sides)
    fold = own_in.shape[1] // 2
    lanes = wave.shape[2]
    bins = lanes // 2
    padded = wave.shape[1] // 2
    inner = cols - 2 * HALF

    me_i = lax.axis_index("inline")
    me_x = lax.axis_index("xline")

    def load(source, target, slot):
        return pltpu.make_async_copy(source, target, local_sem.at[slot])

    load_own = load(traces, own_in, 0)
    load_forward = [load(forward.at[:, group], forward_in.at[:, group], 1 + group) for group in range(GROUPS)]
    base = 1 + GROUPS
    load_filters = load(filters, filters_in, base)
    load_order = load(order, order_in, base + 1)
    load_taps = load(taps, taps_in, base + 2)
    load_first = load(first, first_in, base + 3)
    load_second = load(second.at[me_i if inline_count == 2 else 0], second_in, base + 4)
    load_back = load(back, back_in, base + 5)
    load_inverse = load(inverse, inverse_in, base + 6)
    loads = [load_own, *load_forward, load_filters, load_order, load_taps]
    loads += [load_first, load_second, load_back, load_inverse]
    for each in loads:
        each.start()

    has_left, has_right = me_x > 0, me_x < xline_count - 1
    at_left, at_right = {"xline": me_x - 1}, {"xline": me_x + 1}
    if inline_count == 2:
        bands = [(None, {"inline": 1 - me_i}, (1 - me_i) * (rows - HALF), 0)]
        present = [None]
    elif inline_count > 2:
        has_above, has_below = me_i > 0, me_i < inline_count - 1
        bands = [
            (has_above, {"inline": me_i - 1}, 0, 1),
            (has_below, {"inline": me_i + 1}, rows - HALF, 0),
        ]
        present = [has_above, has_below]
    else:
        bands, present = [], []

    def when(condition, action):
        if condition is None:
            action()
        else:
            pl.when(condition)(action)

    barrier = pltpu.get_barrier_semaphore()
    neighbours = [(has_left, at_left), (has_right, at_right)]
    neighbours += [(exists, where) for exists, where, _, _ in bands]
    for exists, where in neighbours:
        when(exists, lambda: pl.semaphore_signal(barrier, inc=1, device_id=where, device_id_type=MESH))

    def clear(*names):
        for name in names:
            at, size = places[name]
            halo[:, at : at + size, :] = jnp.zeros((GROUPS, size, lanes), F32)

    pl.when(jnp.logical_not(has_left))(lambda: clear("left", *[("from_left", s) for s in range(sides)]))
    pl.when(jnp.logical_not(has_right))(lambda: clear("right", *[("from_right", s) for s in range(sides)]))
    for side, exists in enumerate(present):
        if exists is not None:
            pieces = [(kind, side) for kind in ("low", "high", "middle", "from_left", "from_right")]
            pl.when(jnp.logical_not(exists))(lambda: clear(*pieces))

    slots = {name: slot for slot, name in enumerate(places)}

    def remote(group, name, source, where):
        at, size = places[name]
        slot = group * len(places) + slots[name]
        return pltpu.make_async_remote_copy(
            src_ref=source,
            dst_ref=halo.at[group, pl.ds(at, size)],
            send_sem=send_sem.at[slot],
            recv_sem=recv_sem.at[slot],
            device_id=where,
            device_id_type=MESH,
        )

    def landed(group, name):
        at, size = places[name]
        return halo.at[group, pl.ds(at, size)]

    def come(group, name):
        remote(group, name, landed(group, name), at_left).wait_recv()

    sent = []

    def send(condition, copy):
        when(condition, copy.start)
        sent.append((condition, copy))

    load_own.wait()
    for group in range(GROUPS):
        if group % (GROUPS // 2) == 0:
            if group == 0:
                folded = own_in[:, :fold] + own_in[:, fold:]
            else:
                folded = own_in[:, :fold] - own_in[:, fold:]
            folded = jnp.concatenate(parts(folded), axis=0)
        load_forward[group].wait()
        spectrum = product(folded, forward_in[0, group], forward_in[1, group])
        own[...] = spectrum
        high, low = parts(spectrum)
        own_high[group] = high
        own_low[group] = low
        for row in range(rows):
            at = row * cols
            ends[group, 0, row * HALF : (row + 1) * HALF, :] = own[at : at + HALF, :]
            ends[group, 1, row * HALF : (row + 1) * HALF, :] = own[at + cols - HALF : at + cols, :]
            middle[group, row * inner : (row + 1) * inner, :] = own[at + HALF : at + cols - HALF, :]
        if group == 0:
            peers = sum(1 if exists is None else exists.astype(jnp.int32) for exists, _ in neighbours)
            pl.semaphore_wait(barrier, peers)
        for exists, where, start, side in bands:
            few = pl.ds(pl.multiple_of(start * HALF, HALF * HALF), HALF * HALF)
            many = pl.ds(pl.multiple_of(start * inner, HALF * inner), HALF * inner)
            send(exists, remote(group, ("low", side), ends.at[group, 0, few], where))
            send(exists, remote(group, ("high", side), ends.at[group, 1, few], where))
            send(exists, remote(group, ("middle", side), middle.at[group, many], where))
        send(has_left, remote(group, "right", ends.at[group, 0], at_left))
        send(has_right, remote(group, "left", ends.at[group, 1], at_right))

    def forward_ends(group):
        for side, exists in enumerate(present):
            def on(side=side):
                come(group, ("low", side))
                come(group, ("high", side))
                to_left = remote(group, ("from_right", side), landed(group, ("low", side)), at_left)
                to_right = remote(group, ("from_left", side), landed(group, ("high", side)), at_right)
                pl.when(has_left)(to_left.start)
                pl.when(has_right)(to_right.start)

            when(exists, on)

    def sent_ends(group):
        for side, exists in enumerate(present):
            def on(side=side):
                to_left = remote(group, ("from_right", side), landed(group, ("low", side)), at_left)
                to_right = remote(group, ("from_left", side), landed(group, ("high", side)), at_right)
                pl.when(has_left)(to_left.wait_send)
                pl.when(has_right)(to_right.wait_send)

            when(exists, on)

    load_filters.wait()
    load_order.wait()
    load_taps.wait()
    tap_count = filters_in.shape[0]
    tap_rows[...] = jnp.zeros_like(tap_rows)
    for part in range(2):
        tap_rows[part, :tap_count, :] = filters_in[:, part, :]
    real, imag = parts(tap_rows[0]), parts(tap_rows[1])
    ordered = jnp.dot(
        jnp.concatenate((real[0], imag[0], real[1], imag[1]), axis=0), order_in[...], preferred_element_type=F32
    ).astype(BF16)
    for group in range(GROUPS):
        mine = slice(group * bins, (group + 1) * bins)
        pieces = [ordered[TAP_ROWS * piece : TAP_ROWS * (piece + 1), mine] for piece in range(4)]
        response[group] = product(
            taps_in[...], jnp.concatenate(pieces[:2], axis=1), jnp.concatenate(pieces[2:], axis=1)
        )
    load_first.wait()
    for group in range(GROUPS):
        wave[group] = product(first_in[...], own_high[group], own_low[group])

    load_second.wait()
    load_back.wait()
    load_inverse.wait()
    forward_ends(0)
    halfway = [None, None]
    for group in range(GROUPS):
        pl.when(has_left)(lambda: come(group, "left"))
        pl.when(has_right)(lambda: come(group, "right"))
        for side, exists in enumerate(present):
            def rest(side=side):
                come(group, ("middle", side))
                pl.when(has_left)(lambda: come(group, ("from_left", side)))
                pl.when(has_right)(lambda: come(group, ("from_right", side)))

            when(exists, rest)
        high, low = parts(halo[group])
        wave[group] += product(second_in[...], high, low)
        if group + 1 < GROUPS:
            forward_ends(group + 1)

        rc, rs = wave[group, :padded, :bins], wave[group, padded:, :bins]
        ic, js = wave[group, :padded, bins:], wave[group, padded:, bins:]
        frc, frs = response[group, :padded, :bins], response[group, padded:, :bins]
        fic, fis = response[group, :padded, bins:], response[group, padded:, bins:]
        outcome = {
            (0, 0): rc * frc + rs * frs - (ic * fic + js * fis),
            (1, 0): rc * frs - rs * frc - (ic * fis - js * fic),
            (0, 1): rc * fic + rs * fis + (ic * frc + js * frs),
            (1, 1): rc * fis - rs * fic + (ic * frs - js * frc),
        }
        for (which, part), value in outcome.items():
            high, low = parts(value)
            kept[0, which * padded : (which + 1) * padded, part * bins : (part + 1) * bins] = high
            kept[1, which * padded : (which + 1) * padded, part * bins : (part + 1) * bins] = low
        filtered = product(back_in[...], kept[0], kept[1])
        filtered = jnp.concatenate(parts(filtered), axis=0)
        piece = product(filtered, inverse_in[0, group], inverse_in[1, group])
        parity = group // (GROUPS // 2)
        halfway[parity] = piece if halfway[parity] is None else halfway[parity] + piece
    out[:, :fold] = halfway[0] + halfway[1]
    out[:, fold:] = halfway[0] - halfway[1]

    for condition, copy in sent:
        when(condition, copy.wait_send)
    for group in range(GROUPS):
        sent_ends(group)


def per_device(traces, filters, inline_count, xline_count):
    rows, cols, samples = traces.shape
    _, frequencies, tap_count = filters.shape
    forward, inverse = temporal_tables(samples, frequencies)
    first, second, taps, back = spatial_tables(rows, cols, inline_count)
    order = np.zeros((frequencies, frequencies), ml_dtypes.bfloat16)
    order[bin_groups(frequencies).reshape(-1), np.arange(frequencies)] = 1.0
    sides = min(inline_count - 1, 2)
    places, around = layout(rows, cols, sides)
    own = rows * cols
    waves = first.shape[0] // 2
    lanes = 2 * frequencies // GROUPS
    tables = (forward, inverse, first, second, taps, back, order)
    operands = [traces.reshape(own, samples), filters.transpose(2, 0, 1)]
    operands += [jnp.asarray(table) for table in tables]
    copies = GROUPS * len(places)
    result = pl.pallas_call(
        functools.partial(kernel, rows, cols, inline_count, xline_count),
        out_shape=jax.ShapeDtypeStruct((own, samples), F32),
        in_specs=[pl.BlockSpec(memory_space=pltpu.HBM)] * len(operands),
        out_specs=pl.BlockSpec(memory_space=pltpu.VMEM),
        scratch_shapes=[
            pltpu.VMEM((own, samples), F32),
            pltpu.VMEM((own, lanes), F32),
            pltpu.VMEM((GROUPS, own, lanes), BF16),
            pltpu.VMEM((GROUPS, own, lanes), BF16),
            pltpu.VMEM((GROUPS, 2, rows * HALF, lanes), F32),
            pltpu.VMEM((GROUPS, rows * (cols - 2 * HALF), lanes), F32),
            pltpu.VMEM((GROUPS, around, lanes), F32),
            pltpu.VMEM((GROUPS, waves, lanes), F32),
            pltpu.VMEM((GROUPS, waves, lanes), F32),
            pltpu.VMEM((2, waves, lanes), BF16),
            pltpu.VMEM((2, TAP_ROWS, frequencies), F32),
            pltpu.VMEM((tap_count, 2, frequencies), F32),
            pltpu.VMEM(forward.shape, BF16),
            pltpu.VMEM(inverse.shape, BF16),
            pltpu.VMEM(first.shape, BF16),
            pltpu.VMEM(second.shape[1:], BF16),
            pltpu.VMEM(taps.shape, BF16),
            pltpu.VMEM(back.shape, BF16),
            pltpu.VMEM(order.shape, BF16),
            pltpu.SemaphoreType.DMA((8 + GROUPS,)),
            pltpu.SemaphoreType.DMA((copies,)),
            pltpu.SemaphoreType.DMA((copies,)),
        ],
        compiler_params=pltpu.CompilerParams(
            collective_id=0, has_side_effects=True, vmem_limit_bytes=48 * 1024 * 1024
        ),
    )(*operands)
    return result.reshape(rows, cols, samples)


def solution(mesh):
    return jax.shard_map(
        functools.partial(
            per_device, inline_count=mesh.shape["inline"], xline_count=mesh.shape["xline"]
        ),
        mesh=mesh,
        in_specs=(P("inline", "xline", None), P()),
        out_specs=P("inline", "xline", None),
        check_vma=False,
    )
```

```python
import functools

import jax
import jax.numpy as jnp
import ml_dtypes
import numpy as np
from jax import lax
from jax.experimental import pallas as pl
from jax.experimental.pallas import tpu as pltpu
from jax.sharding import PartitionSpec as P

HALF = 4
GROUPS = 2
TAP_ROWS = 96
MESH = pl.DeviceIdType.MESH
BF16 = jnp.bfloat16
F32 = jnp.float32


def halves(table):
    high = table.astype(np.float32).astype(ml_dtypes.bfloat16)
    low = (table - high.astype(np.float64)).astype(np.float32).astype(ml_dtypes.bfloat16)
    return np.stack((high, low))


def bin_groups(frequencies):
    order = np.concatenate((np.arange(0, frequencies, 2), np.arange(1, frequencies, 2)))
    return order.reshape(GROUPS, frequencies // GROUPS)


def temporal_tables(samples, frequencies):
    time = np.arange(samples // 2)[:, None]
    forward, inverse = [], []
    for bins in bin_groups(frequencies):
        angle = 2.0 * np.pi * (time * bins[None, :] % samples) / samples
        weight = np.where(bins == 0, 1.0, 2.0)[None, :] / samples
        forward.append(np.concatenate((np.cos(angle), -np.sin(angle)), axis=1))
        inverse.append(np.concatenate((weight * np.cos(angle), -weight * np.sin(angle)), axis=1).T)
    return halves(np.stack(forward)), halves(np.stack(inverse))


def spatial_frequencies(height, width):
    chosen = []
    for row in range(height):
        for col in range(width):
            mirror = ((height - row) % height, (width - col) % width)
            if (row, col) <= mirror:
                chosen.append((row, col, 1.0 if (row, col) == mirror else 2.0))
    return np.array(chosen)


def spatial_basis(waves, padded, height, width, positions):
    positions = np.asarray(positions)
    turns = np.outer(waves[:, 0], positions[:, 0]) / height + np.outer(waves[:, 1], positions[:, 1]) / width
    angle = 2.0 * np.pi * turns
    basis = np.zeros((2 * padded, len(positions)))
    basis[: len(waves)] = np.cos(angle)
    basis[padded : padded + len(waves)] = np.sin(angle)
    return basis


def grid(rows, cols):
    return [(row, col) for row in rows for col in cols]


def stacked(table):
    both = halves(table)
    return np.concatenate((both[0], both[1]), axis=0)


def layout(rows, cols, sides):
    strip, ends, middle = rows * HALF, HALF * HALF, HALF * (cols - 2 * HALF)
    sizes = [("left", strip), ("right", strip)]
    for side in range(sides):
        sizes += [(("low", side), ends), (("high", side), ends), (("middle", side), middle)]
        sizes += [(("from_left", side), ends), (("from_right", side), ends)]
    places, at = {}, 0
    for name, size in sizes:
        places[name] = (at, size)
        at += size
    return places, at


def spatial_tables(rows, cols, inline_count):
    height, width = rows + 2 * HALF, cols + 2 * HALF
    waves = spatial_frequencies(height, width)
    padded = -(-len(waves) // 16) * 16
    basis = functools.partial(spatial_basis, waves, padded, height, width)
    below_zero, above_end = range(-HALF, 0), range(cols, cols + HALF)
    own = grid(range(rows), range(cols))
    above, below = range(-HALF, 0), range(rows, rows + HALF)
    variants = [[below], [above]] if inline_count == 2 else [[above, below]]
    sides = min(inline_count - 1, 2)
    second = []
    for bands in variants:
        places = grid(range(rows), below_zero) + grid(range(rows), above_end)
        for band in bands[:sides]:
            places += grid(band, range(HALF)) + grid(band, range(cols - HALF, cols))
            places += grid(band, range(HALF, cols - HALF))
            places += grid(band, below_zero) + grid(band, above_end)
        second.append(stacked(basis(places)))
    reach = range(-HALF, HALF + 1)
    taps = np.zeros((2 * padded, TAP_ROWS))
    taps[:, : len(reach) ** 2] = basis(grid(reach, reach))
    count = np.zeros((2 * padded, 1))
    count[: len(waves), 0] = waves[:, 2] / (height * width)
    count[padded : padded + len(waves), 0] = -waves[:, 2] / (height * width)
    back = (count * basis(own)).T
    return stacked(basis(own)), np.stack(second), stacked(taps), stacked(back)


def parts(value):
    high = value.astype(BF16)
    return high, (value - high.astype(F32)).astype(BF16)


def product(left, high, low):
    dot = functools.partial(jnp.dot, preferred_element_type=F32)
    count = left.shape[0] // 2
    both = dot(left, high)
    return both[:count] + (both[count:] + dot(left[:count], low))


def kernel(
    rows, cols, inline_count, xline_count,
    traces, filters, forward, inverse, first, second, taps, back, order,
    out,
    own_in, own, own_high, own_low, ends, middle, halo, wave, response, kept, tap_rows,
    filters_in, forward_in, inverse_in, first_in, second_in, taps_in, back_in, order_in,
    local_sem, send_sem, recv_sem,
):
    sides = min(inline_count - 1, 2)
    places, _ = layout(rows, cols, sides)
    fold = own_in.shape[1] // 2
    lanes = wave.shape[2]
    bins = lanes // 2
    padded = wave.shape[1] // 2
    inner = cols - 2 * HALF

    me_i = lax.axis_index("inline")
    me_x = lax.axis_index("xline")

    def load(source, target, slot):
        return pltpu.make_async_copy(source, target, local_sem.at[slot])

    load_own = load(traces, own_in, 0)
    load_forward = [load(forward.at[:, group], forward_in.at[:, group], 1 + group) for group in range(GROUPS)]
    base = 1 + GROUPS
    load_filters = load(filters, filters_in, base)
    load_order = load(order, order_in, base + 1)
    load_taps = load(taps, taps_in, base + 2)
    load_first = load(first, first_in, base + 3)
    load_second = load(second.at[me_i if inline_count == 2 else 0], second_in, base + 4)
    load_back = load(back, back_in, base + 5)
    load_inverse = load(inverse, inverse_in, base + 6)
    loads = [load_own, *load_forward, load_filters, load_order, load_taps]
    loads += [load_first, load_second, load_back, load_inverse]
    for each in loads:
        each.start()

    has_left, has_right = me_x > 0, me_x < xline_count - 1
    at_left, at_right = {"xline": me_x - 1}, {"xline": me_x + 1}
    if inline_count == 2:
        bands = [(None, {"inline": 1 - me_i}, (1 - me_i) * (rows - HALF), 0)]
        present = [None]
    elif inline_count > 2:
        has_above, has_below = me_i > 0, me_i < inline_count - 1
        bands = [
            (has_above, {"inline": me_i - 1}, 0, 1),
            (has_below, {"inline": me_i + 1}, rows - HALF, 0),
        ]
        present = [has_above, has_below]
    else:
        bands, present = [], []

    def when(condition, action):
        if condition is None:
            action()
        else:
            pl.when(condition)(action)

    barrier = pltpu.get_barrier_semaphore()
    neighbours = [(has_left, at_left), (has_right, at_right)]
    neighbours += [(exists, where) for exists, where, _, _ in bands]
    for exists, where in neighbours:
        when(exists, lambda: pl.semaphore_signal(barrier, inc=1, device_id=where, device_id_type=MESH))

    def clear(*names):
        for name in names:
            at, size = places[name]
            halo[:, at : at + size, :] = jnp.zeros((GROUPS, size, lanes), F32)

    pl.when(jnp.logical_not(has_left))(lambda: clear("left", *[("from_left", s) for s in range(sides)]))
    pl.when(jnp.logical_not(has_right))(lambda: clear("right", *[("from_right", s) for s in range(sides)]))
    for side, exists in enumerate(present):
        if exists is not None:
            pieces = [(kind, side) for kind in ("low", "high", "middle", "from_left", "from_right")]
            pl.when(jnp.logical_not(exists))(lambda: clear(*pieces))

    slots = {name: slot for slot, name in enumerate(places)}

    def remote(group, name, source, where):
        at, size = places[name]
        slot = group * len(places) + slots[name]
        return pltpu.make_async_remote_copy(
            src_ref=source,
            dst_ref=halo.at[group, pl.ds(at, size)],
            send_sem=send_sem.at[slot],
            recv_sem=recv_sem.at[slot],
            device_id=where,
            device_id_type=MESH,
        )

    def landed(group, name):
        at, size = places[name]
        return halo.at[group, pl.ds(at, size)]

    def come(group, name):
        remote(group, name, landed(group, name), at_left).wait_recv()

    sent = []

    def send(condition, copy):
        when(condition, copy.start)
        sent.append((condition, copy))

    load_own.wait()
    for group in range(GROUPS):
        if group % (GROUPS // 2) == 0:
            if group == 0:
                folded = own_in[:, :fold] + own_in[:, fold:]
            else:
                folded = own_in[:, :fold] - own_in[:, fold:]
            folded = jnp.concatenate(parts(folded), axis=0)
        load_forward[group].wait()
        spectrum = product(folded, forward_in[0, group], forward_in[1, group])
        own[...] = spectrum
        high, low = parts(spectrum)
        own_high[group] = high
        own_low[group] = low
        for row in range(rows):
            at = row * cols
            ends[group, 0, row * HALF : (row + 1) * HALF, :] = own[at : at + HALF, :]
            ends[group, 1, row * HALF : (row + 1) * HALF, :] = own[at + cols - HALF : at + cols, :]
            middle[group, row * inner : (row + 1) * inner, :] = own[at + HALF : at + cols - HALF, :]
        if group == 0:
            peers = sum(1 if exists is None else exists.astype(jnp.int32) for exists, _ in neighbours)
            pl.semaphore_wait(barrier, peers)
        for exists, where, start, side in bands:
            few = pl.ds(pl.multiple_of(start * HALF, HALF * HALF), HALF * HALF)
            many = pl.ds(pl.multiple_of(start * inner, HALF * inner), HALF * inner)
            send(exists, remote(group, ("low", side), ends.at[group, 0, few], where))
            send(exists, remote(group, ("high", side), ends.at[group, 1, few], where))
            send(exists, remote(group, ("middle", side), middle.at[group, many], where))
        send(has_left, remote(group, "right", ends.at[group, 0], at_left))
        send(has_right, remote(group, "left", ends.at[group, 1], at_right))

    def forward_ends(group):
        for side, exists in enumerate(present):
            def on(side=side):
                come(group, ("low", side))
                come(group, ("high", side))
                to_left = remote(group, ("from_right", side), landed(group, ("low", side)), at_left)
                to_right = remote(group, ("from_left", side), landed(group, ("high", side)), at_right)
                pl.when(has_left)(to_left.start)
                pl.when(has_right)(to_right.start)

            when(exists, on)

    def sent_ends(group):
        for side, exists in enumerate(present):
            def on(side=side):
                to_left = remote(group, ("from_right", side), landed(group, ("low", side)), at_left)
                to_right = remote(group, ("from_left", side), landed(group, ("high", side)), at_right)
                pl.when(has_left)(to_left.wait_send)
                pl.when(has_right)(to_right.wait_send)

            when(exists, on)

    load_filters.wait()
    load_order.wait()
    load_taps.wait()
    tap_count = filters_in.shape[0]
    tap_rows[...] = jnp.zeros_like(tap_rows)
    for part in range(2):
        tap_rows[part, :tap_count, :] = filters_in[:, part, :]
    real, imag = parts(tap_rows[0]), parts(tap_rows[1])
    ordered = jnp.dot(
        jnp.concatenate((real[0], imag[0], real[1], imag[1]), axis=0), order_in[...], preferred_element_type=F32
    ).astype(BF16)
    for group in range(GROUPS):
        mine = slice(group * bins, (group + 1) * bins)
        pieces = [ordered[TAP_ROWS * piece : TAP_ROWS * (piece + 1), mine] for piece in range(4)]
        response[group] = product(
            taps_in[...], jnp.concatenate(pieces[:2], axis=1), jnp.concatenate(pieces[2:], axis=1)
        )
    load_first.wait()
    for group in range(GROUPS):
        wave[group] = product(first_in[...], own_high[group], own_low[group])

    load_second.wait()
    load_back.wait()
    load_inverse.wait()
    forward_ends(0)
    halfway = [None, None]
    for group in range(GROUPS):
        pl.when(has_left)(lambda: come(group, "left"))
        pl.when(has_right)(lambda: come(group, "right"))
        for side, exists in enumerate(present):
            def rest(side=side):
                come(group, ("middle", side))
                pl.when(has_left)(lambda: come(group, ("from_left", side)))
                pl.when(has_right)(lambda: come(group, ("from_right", side)))

            when(exists, rest)
        high, low = parts(halo[group])
        wave[group] += product(second_in[...], high, low)
        if group + 1 < GROUPS:
            forward_ends(group + 1)

        rc, rs = wave[group, :padded, :bins], wave[group, padded:, :bins]
        ic, js = wave[group, :padded, bins:], wave[group, padded:, bins:]
        frc, frs = response[group, :padded, :bins], response[group, padded:, :bins]
        fic, fis = response[group, :padded, bins:], response[group, padded:, bins:]
        outcome = {
            (0, 0): rc * frc + rs * frs - (ic * fic + js * fis),
            (1, 0): rc * frs - rs * frc - (ic * fis - js * fic),
            (0, 1): rc * fic + rs * fis + (ic * frc + js * frs),
            (1, 1): rc * fis - rs * fic + (ic * frs - js * frc),
        }
        for (which, part), value in outcome.items():
            high, low = parts(value)
            kept[0, which * padded : (which + 1) * padded, part * bins : (part + 1) * bins] = high
            kept[1, which * padded : (which + 1) * padded, part * bins : (part + 1) * bins] = low
        filtered = product(back_in[...], kept[0], kept[1])
        filtered = jnp.concatenate(parts(filtered), axis=0)
        piece = product(filtered, inverse_in[0, group], inverse_in[1, group])
        parity = group // (GROUPS // 2)
        halfway[parity] = piece if halfway[parity] is None else halfway[parity] + piece
    out[:, :fold] = halfway[0] + halfway[1]
    out[:, fold:] = halfway[0] - halfway[1]

    for condition, copy in sent:
        when(condition, copy.wait_send)
    for group in range(GROUPS):
        sent_ends(group)


def per_device(traces, filters, inline_count, xline_count):
    rows, cols, samples = traces.shape
    _, frequencies, tap_count = filters.shape
    forward, inverse = temporal_tables(samples, frequencies)
    first, second, taps, back = spatial_tables(rows, cols, inline_count)
    order = np.zeros((frequencies, frequencies), ml_dtypes.bfloat16)
    order[bin_groups(frequencies).reshape(-1), np.arange(frequencies)] = 1.0
    sides = min(inline_count - 1, 2)
    places, around = layout(rows, cols, sides)
    own = rows * cols
    waves = first.shape[0] // 2
    lanes = 2 * frequencies // GROUPS
    tables = (forward, inverse, first, second, taps, back, order)
    operands = [traces.reshape(own, samples), filters.transpose(2, 0, 1)]
    operands += [jnp.asarray(table) for table in tables]
    copies = GROUPS * len(places)
    result = pl.pallas_call(
        functools.partial(kernel, rows, cols, inline_count, xline_count),
        out_shape=jax.ShapeDtypeStruct((own, samples), F32),
        in_specs=[pl.BlockSpec(memory_space=pltpu.HBM)] * len(operands),
        out_specs=pl.BlockSpec(memory_space=pltpu.VMEM),
        scratch_shapes=[
            pltpu.VMEM((own, samples), F32),
            pltpu.VMEM((own, lanes), F32),
            pltpu.VMEM((GROUPS, own, lanes), BF16),
            pltpu.VMEM((GROUPS, own, lanes), BF16),
            pltpu.VMEM((GROUPS, 2, rows * HALF, lanes), F32),
            pltpu.VMEM((GROUPS, rows * (cols - 2 * HALF), lanes), F32),
            pltpu.VMEM((GROUPS, around, lanes), F32),
            pltpu.VMEM((GROUPS, waves, lanes), F32),
            pltpu.VMEM((GROUPS, waves, lanes), F32),
            pltpu.VMEM((2, waves, lanes), BF16),
            pltpu.VMEM((2, TAP_ROWS, frequencies), F32),
            pltpu.VMEM((tap_count, 2, frequencies), F32),
            pltpu.VMEM(forward.shape, BF16),
            pltpu.VMEM(inverse.shape, BF16),
            pltpu.VMEM(first.shape, BF16),
            pltpu.VMEM(second.shape[1:], BF16),
            pltpu.VMEM(taps.shape, BF16),
            pltpu.VMEM(back.shape, BF16),
            pltpu.VMEM(order.shape, BF16),
            pltpu.SemaphoreType.DMA((8 + GROUPS,)),
            pltpu.SemaphoreType.DMA((copies,)),
            pltpu.SemaphoreType.DMA((copies,)),
        ],
        compiler_params=pltpu.CompilerParams(
            collective_id=0, has_side_effects=True, vmem_limit_bytes=60 * 1024 * 1024
        ),
    )(*operands)
    return result.reshape(rows, cols, samples)


def solution(mesh):
    return jax.shard_map(
        functools.partial(
            per_device, inline_count=mesh.shape["inline"], xline_count=mesh.shape["xline"]
        ),
        mesh=mesh,
        in_specs=(P("inline", "xline", None), P()),
        out_specs=P("inline", "xline", None),
        check_vma=False,
    )
```

```python
import functools

import jax
import jax.numpy as jnp
import ml_dtypes
import numpy as np
from jax import lax
from jax.experimental import pallas as pl
from jax.experimental.pallas import tpu as pltpu
from jax.sharding import PartitionSpec as P

HALF = 4
GROUPS = 2
TAP_ROWS = 96
MESH = pl.DeviceIdType.MESH
BF16 = jnp.bfloat16
F32 = jnp.float32


def halves(table):
    high = table.astype(np.float32).astype(ml_dtypes.bfloat16)
    low = (table - high.astype(np.float64)).astype(np.float32).astype(ml_dtypes.bfloat16)
    return np.stack((high, low))


def bin_groups(frequencies):
    order = np.concatenate((np.arange(0, frequencies, 2), np.arange(1, frequencies, 2)))
    return order.reshape(GROUPS, frequencies // GROUPS)


def temporal_tables(samples, frequencies):
    time = np.arange(samples // 2)[:, None]
    forward, inverse = [], []
    for bins in bin_groups(frequencies):
        angle = 2.0 * np.pi * (time * bins[None, :] % samples) / samples
        weight = np.where(bins == 0, 1.0, 2.0)[None, :] / samples
        forward.append(np.concatenate((np.cos(angle), -np.sin(angle)), axis=1))
        inverse.append(np.concatenate((weight * np.cos(angle), -weight * np.sin(angle)), axis=1).T)
    return halves(np.stack(forward)), halves(np.stack(inverse))


def spatial_frequencies(height, width):
    chosen = []
    for row in range(height):
        for col in range(width):
            mirror = ((height - row) % height, (width - col) % width)
            if (row, col) <= mirror:
                chosen.append((row, col, 1.0 if (row, col) == mirror else 2.0))
    return np.array(chosen)


def spatial_basis(waves, padded, height, width, positions):
    positions = np.asarray(positions)
    turns = np.outer(waves[:, 0], positions[:, 0]) / height + np.outer(waves[:, 1], positions[:, 1]) / width
    angle = 2.0 * np.pi * turns
    basis = np.zeros((2 * padded, len(positions)))
    basis[: len(waves)] = np.cos(angle)
    basis[padded : padded + len(waves)] = np.sin(angle)
    return basis


def grid(rows, cols):
    return [(row, col) for row in rows for col in cols]


def stacked(table):
    both = halves(table)
    return np.concatenate((both[0], both[1]), axis=0)


def layout(rows, cols, sides):
    strip, ends, middle = rows * HALF, HALF * HALF, HALF * (cols - 2 * HALF)
    sizes = [("left", strip), ("right", strip)]
    for side in range(sides):
        sizes += [(("low", side), ends), (("high", side), ends), (("middle", side), middle)]
        sizes += [(("from_left", side), ends), (("from_right", side), ends)]
    places, at = {}, 0
    for name, size in sizes:
        places[name] = (at, size)
        at += size
    return places, at


def spatial_tables(rows, cols, inline_count):
    height, width = rows + 2 * HALF, cols + 2 * HALF
    waves = spatial_frequencies(height, width)
    padded = -(-len(waves) // 16) * 16
    basis = functools.partial(spatial_basis, waves, padded, height, width)
    below_zero, above_end = range(-HALF, 0), range(cols, cols + HALF)
    own = grid(range(rows), range(cols))
    above, below = range(-HALF, 0), range(rows, rows + HALF)
    variants = [[below], [above]] if inline_count == 2 else [[above, below]]
    sides = min(inline_count - 1, 2)
    second = []
    for bands in variants:
        places = grid(range(rows), below_zero) + grid(range(rows), above_end)
        for band in bands[:sides]:
            places += grid(band, range(HALF)) + grid(band, range(cols - HALF, cols))
            places += grid(band, range(HALF, cols - HALF))
            places += grid(band, below_zero) + grid(band, above_end)
        second.append(stacked(basis(places)))
    reach = range(-HALF, HALF + 1)
    taps = np.zeros((2 * padded, TAP_ROWS))
    taps[:, : len(reach) ** 2] = basis(grid(reach, reach))
    count = np.zeros((2 * padded, 1))
    count[: len(waves), 0] = waves[:, 2] / (height * width)
    count[padded : padded + len(waves), 0] = -waves[:, 2] / (height * width)
    back = (count * basis(own)).T
    return stacked(basis(own)), np.stack(second), stacked(taps), stacked(back)


def parts(value):
    high = value.astype(BF16)
    return high, (value - high.astype(F32)).astype(BF16)


def product(left, high, low):
    dot = functools.partial(jnp.dot, preferred_element_type=F32)
    count = left.shape[0] // 2
    both = dot(left, high)
    return both[:count] + (both[count:] + dot(left[:count], low))


def kernel(
    rows, cols, inline_count, xline_count,
    traces, filters, forward, inverse, first, second, taps, back, order,
    out,
    own_in, own, own_high, own_low, ends, middle, halo, wave, response, kept, tap_rows,
    filters_in, forward_in, inverse_in, first_in, second_in, taps_in, back_in, order_in,
    local_sem, send_sem, recv_sem,
):
    sides = min(inline_count - 1, 2)
    places, _ = layout(rows, cols, sides)
    fold = own_in.shape[1] // 2
    lanes = wave.shape[2]
    bins = lanes // 2
    padded = wave.shape[1] // 2
    inner = cols - 2 * HALF

    me_i = lax.axis_index("inline")
    me_x = lax.axis_index("xline")

    def load(source, target, slot):
        return pltpu.make_async_copy(source, target, local_sem.at[slot])

    load_own = load(traces, own_in, 0)
    load_forward = [load(forward.at[:, group], forward_in.at[:, group], 1 + group) for group in range(GROUPS)]
    base = 1 + GROUPS
    load_filters = load(filters, filters_in, base)
    load_order = load(order, order_in, base + 1)
    load_taps = load(taps, taps_in, base + 2)
    load_first = load(first, first_in, base + 3)
    load_second = load(second.at[me_i if inline_count == 2 else 0], second_in, base + 4)
    load_back = load(back, back_in, base + 5)
    load_inverse = load(inverse, inverse_in, base + 6)
    loads = [load_own, *load_forward, load_filters, load_order, load_taps]
    loads += [load_first, load_second, load_back, load_inverse]
    for each in loads:
        each.start()

    has_left, has_right = me_x > 0, me_x < xline_count - 1
    at_left, at_right = {"xline": me_x - 1}, {"xline": me_x + 1}
    if inline_count == 2:
        bands = [(None, {"inline": 1 - me_i}, (1 - me_i) * (rows - HALF), 0)]
        present = [None]
    elif inline_count > 2:
        has_above, has_below = me_i > 0, me_i < inline_count - 1
        bands = [
            (has_above, {"inline": me_i - 1}, 0, 1),
            (has_below, {"inline": me_i + 1}, rows - HALF, 0),
        ]
        present = [has_above, has_below]
    else:
        bands, present = [], []

    def when(condition, action):
        if condition is None:
            action()
        else:
            pl.when(condition)(action)

    barrier = pltpu.get_barrier_semaphore()
    neighbours = [(has_left, at_left), (has_right, at_right)]
    neighbours += [(exists, where) for exists, where, _, _ in bands]
    for exists, where in neighbours:
        when(exists, lambda: pl.semaphore_signal(barrier, inc=1, device_id=where, device_id_type=MESH))

    def clear(*names):
        for name in names:
            at, size = places[name]
            halo[:, at : at + size, :] = jnp.zeros((GROUPS, size, lanes), F32)

    pl.when(jnp.logical_not(has_left))(lambda: clear("left", *[("from_left", s) for s in range(sides)]))
    pl.when(jnp.logical_not(has_right))(lambda: clear("right", *[("from_right", s) for s in range(sides)]))
    for side, exists in enumerate(present):
        if exists is not None:
            pieces = [(kind, side) for kind in ("low", "high", "middle", "from_left", "from_right")]
            pl.when(jnp.logical_not(exists))(lambda: clear(*pieces))

    slots = {name: slot for slot, name in enumerate(places)}

    def remote(group, name, source, where):
        at, size = places[name]
        slot = group * len(places) + slots[name]
        return pltpu.make_async_remote_copy(
            src_ref=source,
            dst_ref=halo.at[group, pl.ds(at, size)],
            send_sem=send_sem.at[slot],
            recv_sem=recv_sem.at[slot],
            device_id=where,
            device_id_type=MESH,
        )

    def landed(group, name):
        at, size = places[name]
        return halo.at[group, pl.ds(at, size)]

    def come(group, name):
        remote(group, name, landed(group, name), at_left).wait_recv()

    sent = []

    def send(condition, copy):
        when(condition, copy.start)
        sent.append((condition, copy))

    load_own.wait()
    for group in range(GROUPS):
        if group % (GROUPS // 2) == 0:
            if group == 0:
                folded = own_in[:, :fold] + own_in[:, fold:]
            else:
                folded = own_in[:, :fold] - own_in[:, fold:]
            folded = jnp.concatenate(parts(folded), axis=0)
        load_forward[group].wait()
        spectrum = product(folded, forward_in[0, group], forward_in[1, group])
        own[...] = spectrum
        high, low = parts(spectrum)
        own_high[group] = high
        own_low[group] = low
        for row in range(rows):
            at = row * cols
            ends[group, 0, row * HALF : (row + 1) * HALF, :] = own[at : at + HALF, :]
            ends[group, 1, row * HALF : (row + 1) * HALF, :] = own[at + cols - HALF : at + cols, :]
            middle[group, row * inner : (row + 1) * inner, :] = own[at + HALF : at + cols - HALF, :]
        if group == 0:
            peers = sum(1 if exists is None else exists.astype(jnp.int32) for exists, _ in neighbours)
            pl.semaphore_wait(barrier, peers)
        for exists, where, start, side in bands:
            few = pl.ds(pl.multiple_of(start * HALF, HALF * HALF), HALF * HALF)
            send(exists, remote(group, ("low", side), ends.at[group, 0, few], where))
            send(exists, remote(group, ("high", side), ends.at[group, 1, few], where))
        send(has_left, remote(group, "right", ends.at[group, 0], at_left))
        send(has_right, remote(group, "left", ends.at[group, 1], at_right))
    for group in range(GROUPS):
        for exists, where, start, side in bands:
            many = pl.ds(pl.multiple_of(start * inner, HALF * inner), HALF * inner)
            send(exists, remote(group, ("middle", side), middle.at[group, many], where))

    def forward_ends(group):
        for side, exists in enumerate(present):
            def on(side=side):
                come(group, ("low", side))
                come(group, ("high", side))
                to_left = remote(group, ("from_right", side), landed(group, ("low", side)), at_left)
                to_right = remote(group, ("from_left", side), landed(group, ("high", side)), at_right)
                pl.when(has_left)(to_left.start)
                pl.when(has_right)(to_right.start)

            when(exists, on)

    def sent_ends(group):
        for side, exists in enumerate(present):
            def on(side=side):
                to_left = remote(group, ("from_right", side), landed(group, ("low", side)), at_left)
                to_right = remote(group, ("from_left", side), landed(group, ("high", side)), at_right)
                pl.when(has_left)(to_left.wait_send)
                pl.when(has_right)(to_right.wait_send)

            when(exists, on)

    load_filters.wait()
    load_order.wait()
    load_taps.wait()
    tap_count = filters_in.shape[0]
    tap_rows[...] = jnp.zeros_like(tap_rows)
    for part in range(2):
        tap_rows[part, :tap_count, :] = filters_in[:, part, :]
    real, imag = parts(tap_rows[0]), parts(tap_rows[1])
    ordered = jnp.dot(
        jnp.concatenate((real[0], imag[0], real[1], imag[1]), axis=0), order_in[...], preferred_element_type=F32
    ).astype(BF16)
    for group in range(GROUPS):
        mine = slice(group * bins, (group + 1) * bins)
        pieces = [ordered[TAP_ROWS * piece : TAP_ROWS * (piece + 1), mine] for piece in range(4)]
        response[group] = product(
            taps_in[...], jnp.concatenate(pieces[:2], axis=1), jnp.concatenate(pieces[2:], axis=1)
        )
        if group < GROUPS - 1:
            forward_ends(group)
    load_first.wait()
    for group in range(GROUPS):
        wave[group] = product(first_in[...], own_high[group], own_low[group])
        if group == 0:
            forward_ends(GROUPS - 1)

    load_second.wait()
    load_back.wait()
    load_inverse.wait()
    halfway = [None, None]
    for group in range(GROUPS):
        pl.when(has_left)(lambda: come(group, "left"))
        pl.when(has_right)(lambda: come(group, "right"))
        for side, exists in enumerate(present):
            def rest(side=side):
                come(group, ("middle", side))
                pl.when(has_left)(lambda: come(group, ("from_left", side)))
                pl.when(has_right)(lambda: come(group, ("from_right", side)))

            when(exists, rest)
        high, low = parts(halo[group])
        wave[group] += product(second_in[...], high, low)

        rc, rs = wave[group, :padded, :bins], wave[group, padded:, :bins]
        ic, js = wave[group, :padded, bins:], wave[group, padded:, bins:]
        frc, frs = response[group, :padded, :bins], response[group, padded:, :bins]
        fic, fis = response[group, :padded, bins:], response[group, padded:, bins:]
        outcome = {
            (0, 0): rc * frc + rs * frs - (ic * fic + js * fis),
            (1, 0): rc * frs - rs * frc - (ic * fis - js * fic),
            (0, 1): rc * fic + rs * fis + (ic * frc + js * frs),
            (1, 1): rc * fis - rs * fic + (ic * frs - js * frc),
        }
        for (which, part), value in outcome.items():
            high, low = parts(value)
            kept[0, which * padded : (which + 1) * padded, part * bins : (part + 1) * bins] = high
            kept[1, which * padded : (which + 1) * padded, part * bins : (part + 1) * bins] = low
        filtered = product(back_in[...], kept[0], kept[1])
        filtered = jnp.concatenate(parts(filtered), axis=0)
        piece = product(filtered, inverse_in[0, group], inverse_in[1, group])
        parity = group // (GROUPS // 2)
        halfway[parity] = piece if halfway[parity] is None else halfway[parity] + piece
    out[:, :fold] = halfway[0] + halfway[1]
    out[:, fold:] = halfway[0] - halfway[1]

    for condition, copy in sent:
        when(condition, copy.wait_send)
    for group in range(GROUPS):
        sent_ends(group)


def per_device(traces, filters, inline_count, xline_count):
    rows, cols, samples = traces.shape
    _, frequencies, tap_count = filters.shape
    forward, inverse = temporal_tables(samples, frequencies)
    first, second, taps, back = spatial_tables(rows, cols, inline_count)
    order = np.zeros((frequencies, frequencies), ml_dtypes.bfloat16)
    order[bin_groups(frequencies).reshape(-1), np.arange(frequencies)] = 1.0
    sides = min(inline_count - 1, 2)
    places, around = layout(rows, cols, sides)
    own = rows * cols
    waves = first.shape[0] // 2
    lanes = 2 * frequencies // GROUPS
    tables = (forward, inverse, first, second, taps, back, order)
    operands = [traces.reshape(own, samples), filters.transpose(2, 0, 1)]
    operands += [jnp.asarray(table) for table in tables]
    copies = GROUPS * len(places)
    result = pl.pallas_call(
        functools.partial(kernel, rows, cols, inline_count, xline_count),
        out_shape=jax.ShapeDtypeStruct((own, samples), F32),
        in_specs=[pl.BlockSpec(memory_space=pltpu.HBM)] * len(operands),
        out_specs=pl.BlockSpec(memory_space=pltpu.VMEM),
        scratch_shapes=[
            pltpu.VMEM((own, samples), F32),
            pltpu.VMEM((own, lanes), F32),
            pltpu.VMEM((GROUPS, own, lanes), BF16),
            pltpu.VMEM((GROUPS, own, lanes), BF16),
            pltpu.VMEM((GROUPS, 2, rows * HALF, lanes), F32),
            pltpu.VMEM((GROUPS, rows * (cols - 2 * HALF), lanes), F32),
            pltpu.VMEM((GROUPS, around, lanes), F32),
            pltpu.VMEM((GROUPS, waves, lanes), F32),
            pltpu.VMEM((GROUPS, waves, lanes), F32),
            pltpu.VMEM((2, waves, lanes), BF16),
            pltpu.VMEM((2, TAP_ROWS, frequencies), F32),
            pltpu.VMEM((tap_count, 2, frequencies), F32),
            pltpu.VMEM(forward.shape, BF16),
            pltpu.VMEM(inverse.shape, BF16),
            pltpu.VMEM(first.shape, BF16),
            pltpu.VMEM(second.shape[1:], BF16),
            pltpu.VMEM(taps.shape, BF16),
            pltpu.VMEM(back.shape, BF16),
            pltpu.VMEM(order.shape, BF16),
            pltpu.SemaphoreType.DMA((8 + GROUPS,)),
            pltpu.SemaphoreType.DMA((copies,)),
            pltpu.SemaphoreType.DMA((copies,)),
        ],
        compiler_params=pltpu.CompilerParams(
            collective_id=0, has_side_effects=True, vmem_limit_bytes=60 * 1024 * 1024
        ),
    )(*operands)
    return result.reshape(rows, cols, samples)


def solution(mesh):
    return jax.shard_map(
        functools.partial(
            per_device, inline_count=mesh.shape["inline"], xline_count=mesh.shape["xline"]
        ),
        mesh=mesh,
        in_specs=(P("inline", "xline", None), P()),
        out_specs=P("inline", "xline", None),
        check_vma=False,
    )
```

```python
import functools

import jax
import jax.numpy as jnp
import ml_dtypes
import numpy as np
from jax import lax
from jax.experimental import pallas as pl
from jax.experimental.pallas import tpu as pltpu
from jax.sharding import PartitionSpec as P

HALF = 4
GROUPS = 2
TAP_ROWS = 96
MESH = pl.DeviceIdType.MESH
BF16 = jnp.bfloat16
F32 = jnp.float32


def halves(table):
    high = table.astype(np.float32).astype(ml_dtypes.bfloat16)
    low = (table - high.astype(np.float64)).astype(np.float32).astype(ml_dtypes.bfloat16)
    return np.stack((high, low))


def bin_groups(frequencies):
    order = np.concatenate((np.arange(0, frequencies, 2), np.arange(1, frequencies, 2)))
    return order.reshape(GROUPS, frequencies // GROUPS)


def temporal_tables(samples, frequencies):
    time = np.arange(samples // 2)[:, None]
    forward, inverse = [], []
    for bins in bin_groups(frequencies):
        angle = 2.0 * np.pi * (time * bins[None, :] % samples) / samples
        weight = np.where(bins == 0, 1.0, 2.0)[None, :] / samples
        forward.append(np.concatenate((np.cos(angle), -np.sin(angle)), axis=1))
        inverse.append(np.concatenate((weight * np.cos(angle), -weight * np.sin(angle)), axis=1).T)
    return halves(np.stack(forward)), halves(np.stack(inverse))


def spatial_frequencies(height, width):
    chosen = []
    for row in range(height):
        for col in range(width):
            mirror = ((height - row) % height, (width - col) % width)
            if (row, col) <= mirror:
                chosen.append((row, col, 1.0 if (row, col) == mirror else 2.0))
    return np.array(chosen)


def spatial_basis(waves, padded, height, width, positions):
    positions = np.asarray(positions)
    turns = np.outer(waves[:, 0], positions[:, 0]) / height + np.outer(waves[:, 1], positions[:, 1]) / width
    angle = 2.0 * np.pi * turns
    basis = np.zeros((2 * padded, len(positions)))
    basis[: len(waves)] = np.cos(angle)
    basis[padded : padded + len(waves)] = np.sin(angle)
    return basis


def grid(rows, cols):
    return [(row, col) for row in rows for col in cols]


def stacked(table):
    both = halves(table)
    return np.concatenate((both[0], both[1]), axis=0)


def thrice(table):
    both = halves(table)
    return np.concatenate((both[0], both[0], both[1]), axis=1)


def layout(rows, cols, sides):
    strip, ends, middle = rows * HALF, HALF * HALF, HALF * (cols - 2 * HALF)
    sizes = [("left", strip), ("right", strip)]
    for side in range(sides):
        sizes += [(("low", side), ends), (("high", side), ends), (("middle", side), middle)]
        sizes += [(("from_left", side), ends), (("from_right", side), ends)]
    places, at = {}, 0
    for name, size in sizes:
        places[name] = (at, size)
        at += size
    return places, at


def spatial_tables(rows, cols, inline_count):
    height, width = rows + 2 * HALF, cols + 2 * HALF
    waves = spatial_frequencies(height, width)
    padded = -(-len(waves) // 16) * 16
    basis = functools.partial(spatial_basis, waves, padded, height, width)
    below_zero, above_end = range(-HALF, 0), range(cols, cols + HALF)
    own = grid(range(rows), range(cols))
    above, below = range(-HALF, 0), range(rows, rows + HALF)
    variants = [[below], [above]] if inline_count == 2 else [[above, below]]
    sides = min(inline_count - 1, 2)
    second = []
    for bands in variants:
        places = grid(range(rows), below_zero) + grid(range(rows), above_end)
        for band in bands[:sides]:
            places += grid(band, range(HALF)) + grid(band, range(cols - HALF, cols))
            places += grid(band, range(HALF, cols - HALF))
            places += grid(band, below_zero) + grid(band, above_end)
        second.append(thrice(basis(places)))
    reach = range(-HALF, HALF + 1)
    taps = np.zeros((2 * padded, TAP_ROWS))
    taps[:, : len(reach) ** 2] = basis(grid(reach, reach))
    count = np.zeros((2 * padded, 1))
    count[: len(waves), 0] = waves[:, 2] / (height * width)
    count[padded : padded + len(waves), 0] = -waves[:, 2] / (height * width)
    back = (count * basis(own)).T
    return thrice(basis(own)), np.stack(second), thrice(taps), stacked(back)


def parts(value):
    high = value.astype(BF16)
    return high, (value - high.astype(F32)).astype(BF16)


def product(left, high, low):
    dot = functools.partial(jnp.dot, preferred_element_type=F32)
    count = left.shape[0] // 2
    both = dot(left, high)
    return both[:count] + (both[count:] + dot(left[:count], low))


def summed(left, high, low):
    return jnp.dot(left, jnp.concatenate((high, low, high), axis=0), preferred_element_type=F32)


def kernel(
    rows, cols, inline_count, xline_count,
    traces, filters, forward, inverse, first, second, taps, back, order,
    out,
    own_in, own, own_high, own_low, ends, middle, halo, wave, response, kept, tap_rows,
    filters_in, forward_in, inverse_in, first_in, second_in, taps_in, back_in, order_in,
    local_sem, send_sem, recv_sem,
):
    sides = min(inline_count - 1, 2)
    places, _ = layout(rows, cols, sides)
    fold = own_in.shape[1] // 2
    lanes = wave.shape[2]
    bins = lanes // 2
    padded = wave.shape[1] // 2
    inner = cols - 2 * HALF

    me_i = lax.axis_index("inline")
    me_x = lax.axis_index("xline")

    has_left, has_right = me_x > 0, me_x < xline_count - 1
    at_left, at_right = {"xline": me_x - 1}, {"xline": me_x + 1}
    if inline_count == 2:
        bands = [(None, {"inline": 1 - me_i}, (1 - me_i) * (rows - HALF), 0)]
        present = [None]
    elif inline_count > 2:
        has_above, has_below = me_i > 0, me_i < inline_count - 1
        bands = [
            (has_above, {"inline": me_i - 1}, 0, 1),
            (has_below, {"inline": me_i + 1}, rows - HALF, 0),
        ]
        present = [has_above, has_below]
    else:
        bands, present = [], []

    def when(condition, action):
        if condition is None:
            action()
        else:
            pl.when(condition)(action)

    barrier = pltpu.get_barrier_semaphore()
    neighbours = [(has_left, at_left), (has_right, at_right)]
    neighbours += [(exists, where) for exists, where, _, _ in bands]
    for exists, where in neighbours:
        when(exists, lambda: pl.semaphore_signal(barrier, inc=1, device_id=where, device_id_type=MESH))

    def load(source, target, slot):
        return pltpu.make_async_copy(source, target, local_sem.at[slot])

    load_own = load(traces, own_in, 0)
    load_forward = [load(forward.at[:, group], forward_in.at[:, group], 1 + group) for group in range(GROUPS)]
    base = 1 + GROUPS
    load_filters = load(filters, filters_in, base)
    load_order = load(order, order_in, base + 1)
    load_taps = load(taps, taps_in, base + 2)
    load_first = load(first, first_in, base + 3)
    load_second = load(second.at[me_i if inline_count == 2 else 0], second_in, base + 4)
    load_back = load(back, back_in, base + 5)
    load_inverse = load(inverse, inverse_in, base + 6)
    loads = [load_own, *load_forward, load_filters, load_order, load_taps]
    loads += [load_first, load_second, load_back, load_inverse]
    for each in loads:
        each.start()

    def clear(*names):
        for name in names:
            at, size = places[name]
            halo[:, at : at + size, :] = jnp.zeros((GROUPS, size, lanes), F32)

    pl.when(jnp.logical_not(has_left))(lambda: clear("left", *[("from_left", s) for s in range(sides)]))
    pl.when(jnp.logical_not(has_right))(lambda: clear("right", *[("from_right", s) for s in range(sides)]))
    for side, exists in enumerate(present):
        if exists is not None:
            pieces = [(kind, side) for kind in ("low", "high", "middle", "from_left", "from_right")]
            pl.when(jnp.logical_not(exists))(lambda: clear(*pieces))

    slots = {name: slot for slot, name in enumerate(places)}

    def remote(group, name, source, where):
        at, size = places[name]
        slot = group * len(places) + slots[name]
        return pltpu.make_async_remote_copy(
            src_ref=source,
            dst_ref=halo.at[group, pl.ds(at, size)],
            send_sem=send_sem.at[slot],
            recv_sem=recv_sem.at[slot],
            device_id=where,
            device_id_type=MESH,
        )

    def landed(group, name):
        at, size = places[name]
        return halo.at[group, pl.ds(at, size)]

    def come(group, name):
        remote(group, name, landed(group, name), at_left).wait_recv()

    sent = []

    def send(condition, copy):
        when(condition, copy.start)
        sent.append((condition, copy))

    load_own.wait()
    for group in range(GROUPS):
        if group % (GROUPS // 2) == 0:
            if group == 0:
                folded = own_in[:, :fold] + own_in[:, fold:]
            else:
                folded = own_in[:, :fold] - own_in[:, fold:]
            folded = jnp.concatenate(parts(folded), axis=0)
        load_forward[group].wait()
        spectrum = product(folded, forward_in[0, group], forward_in[1, group])
        own[...] = spectrum
        high, low = parts(spectrum)
        own_high[group] = high
        own_low[group] = low
        for row in range(rows):
            at = row * cols
            ends[group, 0, row * HALF : (row + 1) * HALF, :] = own[at : at + HALF, :]
            ends[group, 1, row * HALF : (row + 1) * HALF, :] = own[at + cols - HALF : at + cols, :]
            middle[group, row * inner : (row + 1) * inner, :] = own[at + HALF : at + cols - HALF, :]
        if group == 0:
            peers = sum(1 if exists is None else exists.astype(jnp.int32) for exists, _ in neighbours)
            pl.semaphore_wait(barrier, peers)
        for exists, where, start, side in bands:
            few = pl.ds(pl.multiple_of(start * HALF, HALF * HALF), HALF * HALF)
            send(exists, remote(group, ("low", side), ends.at[group, 0, few], where))
            send(exists, remote(group, ("high", side), ends.at[group, 1, few], where))
        send(has_left, remote(group, "right", ends.at[group, 0], at_left))
        send(has_right, remote(group, "left", ends.at[group, 1], at_right))
    for group in range(GROUPS):
        for exists, where, start, side in bands:
            many = pl.ds(pl.multiple_of(start * inner, HALF * inner), HALF * inner)
            send(exists, remote(group, ("middle", side), middle.at[group, many], where))

    def forward_ends(group):
        for side, exists in enumerate(present):
            def on(side=side):
                come(group, ("low", side))
                come(group, ("high", side))
                to_left = remote(group, ("from_right", side), landed(group, ("low", side)), at_left)
                to_right = remote(group, ("from_left", side), landed(group, ("high", side)), at_right)
                pl.when(has_left)(to_left.start)
                pl.when(has_right)(to_right.start)

            when(exists, on)

    def sent_ends(group):
        for side, exists in enumerate(present):
            def on(side=side):
                to_left = remote(group, ("from_right", side), landed(group, ("low", side)), at_left)
                to_right = remote(group, ("from_left", side), landed(group, ("high", side)), at_right)
                pl.when(has_left)(to_left.wait_send)
                pl.when(has_right)(to_right.wait_send)

            when(exists, on)

    load_filters.wait()
    load_order.wait()
    load_taps.wait()
    tap_count = filters_in.shape[0]
    tap_rows[...] = jnp.zeros_like(tap_rows)
    for part in range(2):
        tap_rows[part, :tap_count, :] = filters_in[:, part, :]
    real, imag = parts(tap_rows[0]), parts(tap_rows[1])
    ordered = jnp.dot(
        jnp.concatenate((real[0], imag[0], real[1], imag[1]), axis=0), order_in[...], preferred_element_type=F32
    ).astype(BF16)
    for group in range(GROUPS):
        mine = slice(group * bins, (group + 1) * bins)
        pieces = [ordered[TAP_ROWS * piece : TAP_ROWS * (piece + 1), mine] for piece in range(4)]
        response[group] = summed(
            taps_in[...], jnp.concatenate(pieces[:2], axis=1), jnp.concatenate(pieces[2:], axis=1)
        )
        if group < GROUPS - 1:
            forward_ends(group)
    load_first.wait()
    for group in range(GROUPS):
        wave[group] = summed(first_in[...], own_high[group], own_low[group])
        if group == 0:
            forward_ends(GROUPS - 1)

    load_second.wait()
    load_back.wait()
    load_inverse.wait()
    halfway = [None, None]
    for group in range(GROUPS):
        pl.when(has_left)(lambda: come(group, "left"))
        pl.when(has_right)(lambda: come(group, "right"))
        for side, exists in enumerate(present):
            def rest(side=side):
                come(group, ("middle", side))
                pl.when(has_left)(lambda: come(group, ("from_left", side)))
                pl.when(has_right)(lambda: come(group, ("from_right", side)))

            when(exists, rest)
        high, low = parts(halo[group])
        wave[group] += summed(second_in[...], high, low)

        rc, rs = wave[group, :padded, :bins], wave[group, padded:, :bins]
        ic, js = wave[group, :padded, bins:], wave[group, padded:, bins:]
        frc, frs = response[group, :padded, :bins], response[group, padded:, :bins]
        fic, fis = response[group, :padded, bins:], response[group, padded:, bins:]
        outcome = {
            (0, 0): rc * frc + rs * frs - (ic * fic + js * fis),
            (1, 0): rc * frs - rs * frc - (ic * fis - js * fic),
            (0, 1): rc * fic + rs * fis + (ic * frc + js * frs),
            (1, 1): rc * fis - rs * fic + (ic * frs - js * frc),
        }
        for (which, part), value in outcome.items():
            high, low = parts(value)
            kept[0, which * padded : (which + 1) * padded, part * bins : (part + 1) * bins] = high
            kept[1, which * padded : (which + 1) * padded, part * bins : (part + 1) * bins] = low
        filtered = product(back_in[...], kept[0], kept[1])
        filtered = jnp.concatenate(parts(filtered), axis=0)
        piece = product(filtered, inverse_in[0, group], inverse_in[1, group])
        parity = group // (GROUPS // 2)
        halfway[parity] = piece if halfway[parity] is None else halfway[parity] + piece
    out[:, :fold] = halfway[0] + halfway[1]
    out[:, fold:] = halfway[0] - halfway[1]

    for condition, copy in sent:
        when(condition, copy.wait_send)
    for group in range(GROUPS):
        sent_ends(group)


def per_device(traces, filters, inline_count, xline_count):
    rows, cols, samples = traces.shape
    _, frequencies, tap_count = filters.shape
    forward, inverse = temporal_tables(samples, frequencies)
    first, second, taps, back = spatial_tables(rows, cols, inline_count)
    order = np.zeros((frequencies, frequencies), ml_dtypes.bfloat16)
    order[bin_groups(frequencies).reshape(-1), np.arange(frequencies)] = 1.0
    sides = min(inline_count - 1, 2)
    places, around = layout(rows, cols, sides)
    own = rows * cols
    waves = first.shape[0]
    lanes = 2 * frequencies // GROUPS
    tables = (forward, inverse, first, second, taps, back, order)
    operands = [traces.reshape(own, samples), filters.transpose(2, 0, 1)]
    operands += [jnp.asarray(table) for table in tables]
    copies = GROUPS * len(places)
    result = pl.pallas_call(
        functools.partial(kernel, rows, cols, inline_count, xline_count),
        out_shape=jax.ShapeDtypeStruct((own, samples), F32),
        in_specs=[pl.BlockSpec(memory_space=pltpu.HBM)] * len(operands),
        out_specs=pl.BlockSpec(memory_space=pltpu.VMEM),
        scratch_shapes=[
            pltpu.VMEM((own, samples), F32),
            pltpu.VMEM((own, lanes), F32),
            pltpu.VMEM((GROUPS, own, lanes), BF16),
            pltpu.VMEM((GROUPS, own, lanes), BF16),
            pltpu.VMEM((GROUPS, 2, rows * HALF, lanes), F32),
            pltpu.VMEM((GROUPS, rows * (cols - 2 * HALF), lanes), F32),
            pltpu.VMEM((GROUPS, around, lanes), F32),
            pltpu.VMEM((GROUPS, waves, lanes), F32),
            pltpu.VMEM((GROUPS, waves, lanes), F32),
            pltpu.VMEM((2, waves, lanes), BF16),
            pltpu.VMEM((2, TAP_ROWS, frequencies), F32),
            pltpu.VMEM((tap_count, 2, frequencies), F32),
            pltpu.VMEM(forward.shape, BF16),
            pltpu.VMEM(inverse.shape, BF16),
            pltpu.VMEM(first.shape, BF16),
            pltpu.VMEM(second.shape[1:], BF16),
            pltpu.VMEM(taps.shape, BF16),
            pltpu.VMEM(back.shape, BF16),
            pltpu.VMEM(order.shape, BF16),
            pltpu.SemaphoreType.DMA((8 + GROUPS,)),
            pltpu.SemaphoreType.DMA((copies,)),
            pltpu.SemaphoreType.DMA((copies,)),
        ],
        compiler_params=pltpu.CompilerParams(
            collective_id=0, has_side_effects=True, vmem_limit_bytes=60 * 1024 * 1024
        ),
    )(*operands)
    return result.reshape(rows, cols, samples)


def solution(mesh):
    return jax.shard_map(
        functools.partial(
            per_device, inline_count=mesh.shape["inline"], xline_count=mesh.shape["xline"]
        ),
        mesh=mesh,
        in_specs=(P("inline", "xline", None), P()),
        out_specs=P("inline", "xline", None),
        check_vma=False,
    )
```

```python
import functools

import jax
import jax.numpy as jnp
import ml_dtypes
import numpy as np
from jax import lax
from jax.experimental import pallas as pl
from jax.experimental.pallas import tpu as pltpu
from jax.sharding import PartitionSpec as P

HALF = 4
GROUPS = 4
TAP_ROWS = 96
MESH = pl.DeviceIdType.MESH
BF16 = jnp.bfloat16
F32 = jnp.float32


def halves(table):
    high = table.astype(np.float32).astype(ml_dtypes.bfloat16)
    low = (table - high.astype(np.float64)).astype(np.float32).astype(ml_dtypes.bfloat16)
    return np.stack((high, low))


def bin_groups(frequencies):
    order = np.concatenate((np.arange(0, frequencies, 2), np.arange(1, frequencies, 2)))
    return order.reshape(GROUPS, frequencies // GROUPS)


def temporal_tables(samples, frequencies):
    time = np.arange(samples // 2)[:, None]
    forward, inverse = [], []
    for bins in bin_groups(frequencies):
        angle = 2.0 * np.pi * (time * bins[None, :] % samples) / samples
        weight = np.where(bins == 0, 1.0, 2.0)[None, :] / samples
        forward.append(np.concatenate((np.cos(angle), -np.sin(angle)), axis=1))
        inverse.append(np.concatenate((weight * np.cos(angle), -weight * np.sin(angle)), axis=1).T)
    return halves(np.stack(forward)), halves(np.stack(inverse))


def spatial_frequencies(height, width):
    chosen = []
    for row in range(height):
        for col in range(width):
            mirror = ((height - row) % height, (width - col) % width)
            if (row, col) <= mirror:
                chosen.append((row, col, 1.0 if (row, col) == mirror else 2.0))
    return np.array(chosen)


def spatial_basis(waves, padded, height, width, positions):
    positions = np.asarray(positions)
    turns = np.outer(waves[:, 0], positions[:, 0]) / height + np.outer(waves[:, 1], positions[:, 1]) / width
    angle = 2.0 * np.pi * turns
    basis = np.zeros((2 * padded, len(positions)))
    basis[: len(waves)] = np.cos(angle)
    basis[padded : padded + len(waves)] = np.sin(angle)
    return basis


def grid(rows, cols):
    return [(row, col) for row in rows for col in cols]


def stacked(table):
    both = halves(table)
    return np.concatenate((both[0], both[1]), axis=0)


def thrice(table):
    both = halves(table)
    return np.concatenate((both[0], both[0], both[1]), axis=1)


def layout(rows, cols, sides):
    strip, ends, middle = rows * HALF, HALF * HALF, HALF * (cols - 2 * HALF)
    sizes = [("left", strip), ("right", strip)]
    for side in range(sides):
        sizes += [(("low", side), ends), (("high", side), ends), (("middle", side), middle)]
        sizes += [(("from_left", side), ends), (("from_right", side), ends)]
    places, at = {}, 0
    for name, size in sizes:
        places[name] = (at, size)
        at += size
    return places, at


def spatial_tables(rows, cols, inline_count):
    height, width = rows + 2 * HALF, cols + 2 * HALF
    waves = spatial_frequencies(height, width)
    padded = -(-len(waves) // 16) * 16
    basis = functools.partial(spatial_basis, waves, padded, height, width)
    below_zero, above_end = range(-HALF, 0), range(cols, cols + HALF)
    own = grid(range(rows), range(cols))
    above, below = range(-HALF, 0), range(rows, rows + HALF)
    variants = [[below], [above]] if inline_count == 2 else [[above, below]]
    sides = min(inline_count - 1, 2)
    second = []
    for bands in variants:
        places = grid(range(rows), below_zero) + grid(range(rows), above_end)
        for band in bands[:sides]:
            places += grid(band, range(HALF)) + grid(band, range(cols - HALF, cols))
            places += grid(band, range(HALF, cols - HALF))
            places += grid(band, below_zero) + grid(band, above_end)
        second.append(thrice(basis(places)))
    reach = range(-HALF, HALF + 1)
    taps = np.zeros((2 * padded, TAP_ROWS))
    taps[:, : len(reach) ** 2] = basis(grid(reach, reach))
    count = np.zeros((2 * padded, 1))
    count[: len(waves), 0] = waves[:, 2] / (height * width)
    count[padded : padded + len(waves), 0] = -waves[:, 2] / (height * width)
    back = (count * basis(own)).T
    return thrice(basis(own)), np.stack(second), thrice(taps), stacked(back)


def parts(value):
    high = value.astype(BF16)
    return high, (value - high.astype(F32)).astype(BF16)


def product(left, high, low):
    dot = functools.partial(jnp.dot, preferred_element_type=F32)
    count = left.shape[0] // 2
    both = dot(left, high)
    return both[:count] + (both[count:] + dot(left[:count], low))


def summed(left, high, low):
    return jnp.dot(left, jnp.concatenate((high, low, high), axis=0), preferred_element_type=F32)


def kernel(
    rows, cols, inline_count, xline_count,
    traces, filters, forward, inverse, first, second, taps, back, order,
    out,
    own_in, own, own_high, own_low, ends, middle, halo, wave, response, kept, tap_rows,
    filters_in, forward_in, inverse_in, first_in, second_in, taps_in, back_in, order_in,
    local_sem, send_sem, recv_sem,
):
    sides = min(inline_count - 1, 2)
    places, _ = layout(rows, cols, sides)
    fold = own_in.shape[1] // 2
    lanes = wave.shape[2]
    bins = lanes // 2
    padded = wave.shape[1] // 2
    inner = cols - 2 * HALF

    me_i = lax.axis_index("inline")
    me_x = lax.axis_index("xline")

    has_left, has_right = me_x > 0, me_x < xline_count - 1
    at_left, at_right = {"xline": me_x - 1}, {"xline": me_x + 1}
    if inline_count == 2:
        bands = [(None, {"inline": 1 - me_i}, (1 - me_i) * (rows - HALF), 0)]
        present = [None]
    elif inline_count > 2:
        has_above, has_below = me_i > 0, me_i < inline_count - 1
        bands = [
            (has_above, {"inline": me_i - 1}, 0, 1),
            (has_below, {"inline": me_i + 1}, rows - HALF, 0),
        ]
        present = [has_above, has_below]
    else:
        bands, present = [], []

    def when(condition, action):
        if condition is None:
            action()
        else:
            pl.when(condition)(action)

    barrier = pltpu.get_barrier_semaphore()
    neighbours = [(has_left, at_left), (has_right, at_right)]
    neighbours += [(exists, where) for exists, where, _, _ in bands]
    for exists, where in neighbours:
        when(exists, lambda: pl.semaphore_signal(barrier, inc=1, device_id=where, device_id_type=MESH))

    def load(source, target, slot):
        return pltpu.make_async_copy(source, target, local_sem.at[slot])

    load_own = load(traces, own_in, 0)
    load_forward = [load(forward.at[:, group], forward_in.at[:, group], 1 + group) for group in range(GROUPS)]
    base = 1 + GROUPS
    load_filters = load(filters, filters_in, base)
    load_order = load(order, order_in, base + 1)
    load_taps = load(taps, taps_in, base + 2)
    load_first = load(first, first_in, base + 3)
    load_second = load(second.at[me_i if inline_count == 2 else 0], second_in, base + 4)
    load_back = load(back, back_in, base + 5)
    load_inverse = load(inverse, inverse_in, base + 6)
    loads = [load_own, *load_forward, load_filters, load_order, load_taps]
    loads += [load_first, load_second, load_back, load_inverse]
    for each in loads:
        each.start()

    def clear(*names):
        for name in names:
            at, size = places[name]
            halo[:, at : at + size, :] = jnp.zeros((GROUPS, size, lanes), F32)

    pl.when(jnp.logical_not(has_left))(lambda: clear("left", *[("from_left", s) for s in range(sides)]))
    pl.when(jnp.logical_not(has_right))(lambda: clear("right", *[("from_right", s) for s in range(sides)]))
    for side, exists in enumerate(present):
        if exists is not None:
            pieces = [(kind, side) for kind in ("low", "high", "middle", "from_left", "from_right")]
            pl.when(jnp.logical_not(exists))(lambda: clear(*pieces))

    slots = {name: slot for slot, name in enumerate(places)}

    def remote(group, name, source, where):
        at, size = places[name]
        slot = group * len(places) + slots[name]
        return pltpu.make_async_remote_copy(
            src_ref=source,
            dst_ref=halo.at[group, pl.ds(at, size)],
            send_sem=send_sem.at[slot],
            recv_sem=recv_sem.at[slot],
            device_id=where,
            device_id_type=MESH,
        )

    def landed(group, name):
        at, size = places[name]
        return halo.at[group, pl.ds(at, size)]

    def come(group, name):
        remote(group, name, landed(group, name), at_left).wait_recv()

    sent = []

    def send(condition, copy):
        when(condition, copy.start)
        sent.append((condition, copy))

    load_own.wait()
    for group in range(GROUPS):
        if group % (GROUPS // 2) == 0:
            if group == 0:
                folded = own_in[:, :fold] + own_in[:, fold:]
            else:
                folded = own_in[:, :fold] - own_in[:, fold:]
            folded = jnp.concatenate(parts(folded), axis=0)
        load_forward[group].wait()
        spectrum = product(folded, forward_in[0, group], forward_in[1, group])
        own[...] = spectrum
        high, low = parts(spectrum)
        own_high[group] = high
        own_low[group] = low
        for row in range(rows):
            at = row * cols
            ends[group, 0, row * HALF : (row + 1) * HALF, :] = own[at : at + HALF, :]
            ends[group, 1, row * HALF : (row + 1) * HALF, :] = own[at + cols - HALF : at + cols, :]
            middle[group, row * inner : (row + 1) * inner, :] = own[at + HALF : at + cols - HALF, :]
        if group == 0:
            peers = sum(1 if exists is None else exists.astype(jnp.int32) for exists, _ in neighbours)
            pl.semaphore_wait(barrier, peers)
        for exists, where, start, side in bands:
            few = pl.ds(pl.multiple_of(start * HALF, HALF * HALF), HALF * HALF)
            send(exists, remote(group, ("low", side), ends.at[group, 0, few], where))
            send(exists, remote(group, ("high", side), ends.at[group, 1, few], where))
        send(has_left, remote(group, "right", ends.at[group, 0], at_left))
        send(has_right, remote(group, "left", ends.at[group, 1], at_right))
    for group in range(GROUPS):
        for exists, where, start, side in bands:
            many = pl.ds(pl.multiple_of(start * inner, HALF * inner), HALF * inner)
            send(exists, remote(group, ("middle", side), middle.at[group, many], where))

    def forward_ends(group):
        for side, exists in enumerate(present):
            def on(side=side):
                come(group, ("low", side))
                come(group, ("high", side))
                to_left = remote(group, ("from_right", side), landed(group, ("low", side)), at_left)
                to_right = remote(group, ("from_left", side), landed(group, ("high", side)), at_right)
                pl.when(has_left)(to_left.start)
                pl.when(has_right)(to_right.start)

            when(exists, on)

    def sent_ends(group):
        for side, exists in enumerate(present):
            def on(side=side):
                to_left = remote(group, ("from_right", side), landed(group, ("low", side)), at_left)
                to_right = remote(group, ("from_left", side), landed(group, ("high", side)), at_right)
                pl.when(has_left)(to_left.wait_send)
                pl.when(has_right)(to_right.wait_send)

            when(exists, on)

    load_filters.wait()
    load_order.wait()
    load_taps.wait()
    tap_count = filters_in.shape[0]
    tap_rows[...] = jnp.zeros_like(tap_rows)
    for part in range(2):
        tap_rows[part, :tap_count, :] = filters_in[:, part, :]
    real, imag = parts(tap_rows[0]), parts(tap_rows[1])
    ordered = jnp.dot(
        jnp.concatenate((real[0], imag[0], real[1], imag[1]), axis=0), order_in[...], preferred_element_type=F32
    ).astype(BF16)
    for group in range(GROUPS):
        mine = slice(group * bins, (group + 1) * bins)
        pieces = [ordered[TAP_ROWS * piece : TAP_ROWS * (piece + 1), mine] for piece in range(4)]
        response[group] = summed(
            taps_in[...], jnp.concatenate(pieces[:2], axis=1), jnp.concatenate(pieces[2:], axis=1)
        )
        if group < GROUPS - 1:
            forward_ends(group)
    load_first.wait()
    for group in range(GROUPS):
        wave[group] = summed(first_in[...], own_high[group], own_low[group])
        if group == 0:
            forward_ends(GROUPS - 1)

    load_second.wait()
    load_back.wait()
    load_inverse.wait()
    halfway = [None, None]
    for group in range(GROUPS):
        pl.when(has_left)(lambda: come(group, "left"))
        pl.when(has_right)(lambda: come(group, "right"))
        for side, exists in enumerate(present):
            def rest(side=side):
                come(group, ("middle", side))
                pl.when(has_left)(lambda: come(group, ("from_left", side)))
                pl.when(has_right)(lambda: come(group, ("from_right", side)))

            when(exists, rest)
        high, low = parts(halo[group])
        wave[group] += summed(second_in[...], high, low)

        rc, rs = wave[group, :padded, :bins], wave[group, padded:, :bins]
        ic, js = wave[group, :padded, bins:], wave[group, padded:, bins:]
        frc, frs = response[group, :padded, :bins], response[group, padded:, :bins]
        fic, fis = response[group, :padded, bins:], response[group, padded:, bins:]
        outcome = {
            (0, 0): rc * frc + rs * frs - (ic * fic + js * fis),
            (1, 0): rc * frs - rs * frc - (ic * fis - js * fic),
            (0, 1): rc * fic + rs * fis + (ic * frc + js * frs),
            (1, 1): rc * fis - rs * fic + (ic * frs - js * frc),
        }
        for (which, part), value in outcome.items():
            high, low = parts(value)
            kept[0, which * padded : (which + 1) * padded, part * bins : (part + 1) * bins] = high
            kept[1, which * padded : (which + 1) * padded, part * bins : (part + 1) * bins] = low
        filtered = product(back_in[...], kept[0], kept[1])
        filtered = jnp.concatenate(parts(filtered), axis=0)
        piece = product(filtered, inverse_in[0, group], inverse_in[1, group])
        parity = group // (GROUPS // 2)
        halfway[parity] = piece if halfway[parity] is None else halfway[parity] + piece
    out[:, :fold] = halfway[0] + halfway[1]
    out[:, fold:] = halfway[0] - halfway[1]

    for condition, copy in sent:
        when(condition, copy.wait_send)
    for group in range(GROUPS):
        sent_ends(group)


def per_device(traces, filters, inline_count, xline_count):
    rows, cols, samples = traces.shape
    _, frequencies, tap_count = filters.shape
    forward, inverse = temporal_tables(samples, frequencies)
    first, second, taps, back = spatial_tables(rows, cols, inline_count)
    order = np.zeros((frequencies, frequencies), ml_dtypes.bfloat16)
    order[bin_groups(frequencies).reshape(-1), np.arange(frequencies)] = 1.0
    sides = min(inline_count - 1, 2)
    places, around = layout(rows, cols, sides)
    own = rows * cols
    waves = first.shape[0]
    lanes = 2 * frequencies // GROUPS
    tables = (forward, inverse, first, second, taps, back, order)
    operands = [traces.reshape(own, samples), filters.transpose(2, 0, 1)]
    operands += [jnp.asarray(table) for table in tables]
    copies = GROUPS * len(places)
    result = pl.pallas_call(
        functools.partial(kernel, rows, cols, inline_count, xline_count),
        out_shape=jax.ShapeDtypeStruct((own, samples), F32),
        in_specs=[pl.BlockSpec(memory_space=pltpu.HBM)] * len(operands),
        out_specs=pl.BlockSpec(memory_space=pltpu.VMEM),
        scratch_shapes=[
            pltpu.VMEM((own, samples), F32),
            pltpu.VMEM((own, lanes), F32),
            pltpu.VMEM((GROUPS, own, lanes), BF16),
            pltpu.VMEM((GROUPS, own, lanes), BF16),
            pltpu.VMEM((GROUPS, 2, rows * HALF, lanes), F32),
            pltpu.VMEM((GROUPS, rows * (cols - 2 * HALF), lanes), F32),
            pltpu.VMEM((GROUPS, around, lanes), F32),
            pltpu.VMEM((GROUPS, waves, lanes), F32),
            pltpu.VMEM((GROUPS, waves, lanes), F32),
            pltpu.VMEM((2, waves, lanes), BF16),
            pltpu.VMEM((2, TAP_ROWS, frequencies), F32),
            pltpu.VMEM((tap_count, 2, frequencies), F32),
            pltpu.VMEM(forward.shape, BF16),
            pltpu.VMEM(inverse.shape, BF16),
            pltpu.VMEM(first.shape, BF16),
            pltpu.VMEM(second.shape[1:], BF16),
            pltpu.VMEM(taps.shape, BF16),
            pltpu.VMEM(back.shape, BF16),
            pltpu.VMEM(order.shape, BF16),
            pltpu.SemaphoreType.DMA((8 + GROUPS,)),
            pltpu.SemaphoreType.DMA((copies,)),
            pltpu.SemaphoreType.DMA((copies,)),
        ],
        compiler_params=pltpu.CompilerParams(
            collective_id=0, has_side_effects=True, vmem_limit_bytes=60 * 1024 * 1024
        ),
    )(*operands)
    return result.reshape(rows, cols, samples)


def solution(mesh):
    return jax.shard_map(
        functools.partial(
            per_device, inline_count=mesh.shape["inline"], xline_count=mesh.shape["xline"]
        ),
        mesh=mesh,
        in_specs=(P("inline", "xline", None), P()),
        out_specs=P("inline", "xline", None),
        check_vma=False,
    )
```

```python
import functools

import jax
import jax.numpy as jnp
import ml_dtypes
import numpy as np
from jax import lax
from jax.experimental import pallas as pl
from jax.experimental.pallas import tpu as pltpu
from jax.sharding import PartitionSpec as P

HALF = 4
GROUPS = 2
TAP_ROWS = 96
PIECES = 4
MESH = pl.DeviceIdType.MESH
BF16 = jnp.bfloat16
F32 = jnp.float32


def halves(table):
    high = table.astype(np.float32).astype(ml_dtypes.bfloat16)
    low = (table - high.astype(np.float64)).astype(np.float32).astype(ml_dtypes.bfloat16)
    return np.stack((high, low))


def bin_groups(frequencies):
    order = np.concatenate((np.arange(0, frequencies, 2), np.arange(1, frequencies, 2)))
    return order.reshape(GROUPS, frequencies // GROUPS)


def temporal_tables(samples, frequencies):
    time = np.arange(samples // 2)[:, None]
    forward, inverse = [], []
    for bins in bin_groups(frequencies):
        angle = 2.0 * np.pi * (time * bins[None, :] % samples) / samples
        weight = np.where(bins == 0, 1.0, 2.0)[None, :] / samples
        forward.append(np.concatenate((np.cos(angle), -np.sin(angle)), axis=1))
        inverse.append(np.concatenate((weight * np.cos(angle), -weight * np.sin(angle)), axis=1).T)
    return halves(np.stack(forward)), halves(np.stack(inverse))


def spatial_frequencies(height, width):
    chosen = []
    for row in range(height):
        for col in range(width):
            mirror = ((height - row) % height, (width - col) % width)
            if (row, col) <= mirror:
                chosen.append((row, col, 1.0 if (row, col) == mirror else 2.0))
    return np.array(chosen)


def spatial_basis(waves, padded, height, width, positions):
    positions = np.asarray(positions)
    turns = np.outer(waves[:, 0], positions[:, 0]) / height + np.outer(waves[:, 1], positions[:, 1]) / width
    angle = 2.0 * np.pi * turns
    basis = np.zeros((2 * padded, len(positions)))
    basis[: len(waves)] = np.cos(angle)
    basis[padded : padded + len(waves)] = np.sin(angle)
    return basis


def grid(rows, cols):
    return [(row, col) for row in rows for col in cols]


def stacked(table):
    both = halves(table)
    return np.concatenate((both[0], both[1]), axis=0)


def thrice(table):
    both = halves(table)
    return np.concatenate((both[0], both[0], both[1]), axis=1)


def layout(rows, cols, sides):
    strip, ends, middle = rows * HALF, HALF * HALF, HALF * (cols - 2 * HALF)
    sizes = [("left", strip), ("right", strip)]
    for side in range(sides):
        sizes += [(("low", side), ends), (("high", side), ends), (("middle", side), middle)]
        sizes += [(("from_left", side), ends), (("from_right", side), ends)]
    places, at = {}, 0
    for name, size in sizes:
        places[name] = (at, size)
        at += size
    return places, at


def spatial_tables(rows, cols, inline_count):
    height, width = rows + 2 * HALF, cols + 2 * HALF
    waves = spatial_frequencies(height, width)
    padded = -(-len(waves) // 16) * 16
    basis = functools.partial(spatial_basis, waves, padded, height, width)
    below_zero, above_end = range(-HALF, 0), range(cols, cols + HALF)
    own = grid(range(rows), range(cols))
    above, below = range(-HALF, 0), range(rows, rows + HALF)
    variants = [[below], [above]] if inline_count == 2 else [[above, below]]
    sides = min(inline_count - 1, 2)
    second = []
    for bands in variants:
        places = grid(range(rows), below_zero) + grid(range(rows), above_end)
        for band in bands[:sides]:
            places += grid(band, range(HALF)) + grid(band, range(cols - HALF, cols))
            places += grid(band, range(HALF, cols - HALF))
            places += grid(band, below_zero) + grid(band, above_end)
        second.append(thrice(basis(places)))
    reach = range(-HALF, HALF + 1)
    taps = np.zeros((2 * padded, TAP_ROWS))
    taps[:, : len(reach) ** 2] = basis(grid(reach, reach))
    count = np.zeros((2 * padded, 1))
    count[: len(waves), 0] = waves[:, 2] / (height * width)
    count[padded : padded + len(waves), 0] = -waves[:, 2] / (height * width)
    back = (count * basis(own)).T
    return thrice(basis(own)), np.stack(second), thrice(taps), stacked(back)


def parts(value):
    high = value.astype(BF16)
    return high, (value - high.astype(F32)).astype(BF16)


def product(left, high, low):
    dot = functools.partial(jnp.dot, preferred_element_type=F32)
    count = left.shape[0] // 2
    both = dot(left, high)
    return both[:count] + (both[count:] + dot(left[:count], low))


def summed(left, high, low):
    return jnp.dot(left, jnp.concatenate((high, low, high), axis=0), preferred_element_type=F32)


def kernel(
    rows, cols, inline_count, xline_count,
    traces, filters, forward, inverse, first, second, taps, back, order,
    out,
    own_in, own, own_high, own_low, ends, middle, halo, wave, response, kept, tap_rows,
    filters_in, forward_in, inverse_in, first_in, second_in, taps_in, back_in, order_in,
    local_sem, send_sem, recv_sem,
):
    sides = min(inline_count - 1, 2)
    places, _ = layout(rows, cols, sides)
    fold = own_in.shape[1] // 2
    lanes = wave.shape[2]
    bins = lanes // 2
    padded = wave.shape[1] // 2
    inner = cols - 2 * HALF

    me_i = lax.axis_index("inline")
    me_x = lax.axis_index("xline")

    has_left, has_right = me_x > 0, me_x < xline_count - 1
    at_left, at_right = {"xline": me_x - 1}, {"xline": me_x + 1}
    if inline_count == 2:
        bands = [(None, {"inline": 1 - me_i}, (1 - me_i) * (rows - HALF), 0)]
        present = [None]
    elif inline_count > 2:
        has_above, has_below = me_i > 0, me_i < inline_count - 1
        bands = [
            (has_above, {"inline": me_i - 1}, 0, 1),
            (has_below, {"inline": me_i + 1}, rows - HALF, 0),
        ]
        present = [has_above, has_below]
    else:
        bands, present = [], []

    def when(condition, action):
        if condition is None:
            action()
        else:
            pl.when(condition)(action)

    barrier = pltpu.get_barrier_semaphore()
    neighbours = [(has_left, at_left), (has_right, at_right)]
    neighbours += [(exists, where) for exists, where, _, _ in bands]
    for exists, where in neighbours:
        when(exists, lambda: pl.semaphore_signal(barrier, inc=1, device_id=where, device_id_type=MESH))

    def load(source, target, slot):
        return pltpu.make_async_copy(source, target, local_sem.at[slot])

    load_own = load(traces, own_in, 0)
    load_forward = [load(forward.at[:, group], forward_in.at[:, group], 1 + group) for group in range(GROUPS)]
    base = 1 + GROUPS
    load_filters = load(filters, filters_in, base)
    load_order = load(order, order_in, base + 1)
    load_taps = load(taps, taps_in, base + 2)
    load_first = load(first, first_in, base + 3)
    load_second = load(second.at[me_i if inline_count == 2 else 0], second_in, base + 4)
    load_back = load(back, back_in, base + 5)
    load_inverse = load(inverse, inverse_in, base + 6)
    loads = [load_own, *load_forward, load_filters, load_order, load_taps]
    loads += [load_first, load_second, load_back, load_inverse]
    for each in loads:
        each.start()

    def clear(*names):
        for name in names:
            at, size = places[name]
            halo[:, at : at + size, :] = jnp.zeros((GROUPS, size, lanes), F32)

    pl.when(jnp.logical_not(has_left))(lambda: clear("left", *[("from_left", s) for s in range(sides)]))
    pl.when(jnp.logical_not(has_right))(lambda: clear("right", *[("from_right", s) for s in range(sides)]))
    for side, exists in enumerate(present):
        if exists is not None:
            pieces = [(kind, side) for kind in ("low", "high", "middle", "from_left", "from_right")]
            pl.when(jnp.logical_not(exists))(lambda: clear(*pieces))

    slots = {name: slot for slot, name in enumerate(places)}

    def remote(group, name, source, where):
        at, size = places[name]
        slot = group * len(places) + slots[name]
        return pltpu.make_async_remote_copy(
            src_ref=source,
            dst_ref=halo.at[group, pl.ds(at, size)],
            send_sem=send_sem.at[slot],
            recv_sem=recv_sem.at[slot],
            device_id=where,
            device_id_type=MESH,
        )

    def landed(group, name):
        at, size = places[name]
        return halo.at[group, pl.ds(at, size)]

    def come(group, name):
        remote(group, name, landed(group, name), at_left).wait_recv()

    sent = []

    def send(condition, copy):
        when(condition, copy.start)
        sent.append((condition, copy))

    load_own.wait()
    for group in range(GROUPS):
        if group % (GROUPS // 2) == 0:
            if group == 0:
                folded = own_in[:, :fold] + own_in[:, fold:]
            else:
                folded = own_in[:, :fold] - own_in[:, fold:]
            folded = jnp.concatenate(parts(folded), axis=0)
        load_forward[group].wait()
        spectrum = product(folded, forward_in[0, group], forward_in[1, group])
        own[...] = spectrum
        high, low = parts(spectrum)
        own_high[group] = high
        own_low[group] = low
        for row in range(rows):
            at = row * cols
            ends[group, 0, row * HALF : (row + 1) * HALF, :] = own[at : at + HALF, :]
            ends[group, 1, row * HALF : (row + 1) * HALF, :] = own[at + cols - HALF : at + cols, :]
            middle[group, row * inner : (row + 1) * inner, :] = own[at + HALF : at + cols - HALF, :]
        if group == 0:
            peers = sum(1 if exists is None else exists.astype(jnp.int32) for exists, _ in neighbours)
            pl.semaphore_wait(barrier, peers)
        for exists, where, start, side in bands:
            few = pl.ds(pl.multiple_of(start * HALF, HALF * HALF), HALF * HALF)
            send(exists, remote(group, ("low", side), ends.at[group, 0, few], where))
            send(exists, remote(group, ("high", side), ends.at[group, 1, few], where))
        send(has_left, remote(group, "right", ends.at[group, 0], at_left))
        send(has_right, remote(group, "left", ends.at[group, 1], at_right))
        for exists, where, start, side in bands:
            many = pl.ds(pl.multiple_of(start * inner, HALF * inner), HALF * inner)
            send(exists, remote(group, ("middle", side), middle.at[group, many], where))

    def forward_ends(group):
        for side, exists in enumerate(present):
            def on(side=side):
                come(group, ("low", side))
                come(group, ("high", side))
                to_left = remote(group, ("from_right", side), landed(group, ("low", side)), at_left)
                to_right = remote(group, ("from_left", side), landed(group, ("high", side)), at_right)
                pl.when(has_left)(to_left.start)
                pl.when(has_right)(to_right.start)

            when(exists, on)

    def sent_ends(group):
        for side, exists in enumerate(present):
            def on(side=side):
                to_left = remote(group, ("from_right", side), landed(group, ("low", side)), at_left)
                to_right = remote(group, ("from_left", side), landed(group, ("high", side)), at_right)
                pl.when(has_left)(to_left.wait_send)
                pl.when(has_right)(to_right.wait_send)

            when(exists, on)

    load_filters.wait()
    load_order.wait()
    load_taps.wait()
    tap_count = filters_in.shape[0]
    tap_rows[...] = jnp.zeros_like(tap_rows)
    for part in range(2):
        tap_rows[part, :tap_count, :] = filters_in[:, part, :]
    real, imag = parts(tap_rows[0]), parts(tap_rows[1])
    ordered = jnp.dot(
        jnp.concatenate((real[0], imag[0], real[1], imag[1]), axis=0), order_in[...], preferred_element_type=F32
    ).astype(BF16)
    for group in range(GROUPS):
        mine = slice(group * bins, (group + 1) * bins)
        pieces = [ordered[TAP_ROWS * piece : TAP_ROWS * (piece + 1), mine] for piece in range(4)]
        response[group] = summed(
            taps_in[...], jnp.concatenate(pieces[:2], axis=1), jnp.concatenate(pieces[2:], axis=1)
        )
    forward_ends(0)
    load_first.wait()
    for group in range(GROUPS):
        wave[group] = summed(first_in[...], own_high[group], own_low[group])

    load_second.wait()
    load_back.wait()
    load_inverse.wait()
    halfway = [None, None]
    for group in range(GROUPS):
        pl.when(has_left)(lambda: come(group, "left"))
        pl.when(has_right)(lambda: come(group, "right"))
        for side, exists in enumerate(present):
            def rest(side=side):
                come(group, ("middle", side))
                pl.when(has_left)(lambda: come(group, ("from_left", side)))
                pl.when(has_right)(lambda: come(group, ("from_right", side)))

            when(exists, rest)
        high, low = parts(halo[group])
        wave[group] += summed(second_in[...], high, low)

        rc, rs = wave[group, :padded, :bins], wave[group, padded:, :bins]
        ic, js = wave[group, :padded, bins:], wave[group, padded:, bins:]
        frc, frs = response[group, :padded, :bins], response[group, padded:, :bins]
        fic, fis = response[group, :padded, bins:], response[group, padded:, bins:]
        outcome = {
            (0, 0): rc * frc + rs * frs - (ic * fic + js * fis),
            (1, 0): rc * frs - rs * frc - (ic * fis - js * fic),
            (0, 1): rc * fic + rs * fis + (ic * frc + js * frs),
            (1, 1): rc * fis - rs * fic + (ic * frs - js * frc),
        }
        for (which, part), value in outcome.items():
            high, low = parts(value)
            kept[0, which * padded : (which + 1) * padded, part * bins : (part + 1) * bins] = high
            kept[1, which * padded : (which + 1) * padded, part * bins : (part + 1) * bins] = low
        if group + 1 < GROUPS:
            forward_ends(group + 1)
        filtered = product(back_in[...], kept[0], kept[1])
        filtered = jnp.concatenate(parts(filtered), axis=0)
        piece = product(filtered, inverse_in[0, group], inverse_in[1, group])
        parity = group // (GROUPS // 2)
        halfway[parity] = piece if halfway[parity] is None else halfway[parity] + piece
    out[:, :fold] = halfway[0] + halfway[1]
    out[:, fold:] = halfway[0] - halfway[1]

    for condition, copy in sent:
        when(condition, copy.wait_send)
    for group in range(GROUPS):
        sent_ends(group)


def pass_on(rows, source, target, sem):
    size = rows // PIECES
    pieces = [pl.ds(piece * size, size) for piece in range(PIECES)]
    copies = [
        pltpu.make_async_copy(source.at[piece], target.at[piece], sem.at[slot])
        for slot, piece in enumerate(pieces)
    ]
    for copy in copies:
        copy.start()
    for copy in copies:
        copy.wait()


def per_device(traces, filters, inline_count, xline_count):
    rows, cols, samples = traces.shape
    _, frequencies, tap_count = filters.shape
    forward, inverse = temporal_tables(samples, frequencies)
    first, second, taps, back = spatial_tables(rows, cols, inline_count)
    order = np.zeros((frequencies, frequencies), ml_dtypes.bfloat16)
    order[bin_groups(frequencies).reshape(-1), np.arange(frequencies)] = 1.0
    sides = min(inline_count - 1, 2)
    places, around = layout(rows, cols, sides)
    own = rows * cols
    waves = first.shape[0]
    lanes = 2 * frequencies // GROUPS
    tables = (forward, inverse, first, second, taps, back, order)
    operands = [traces.reshape(own, samples), filters.transpose(2, 0, 1)]
    operands += [jnp.asarray(table) for table in tables]
    copies = GROUPS * len(places)
    result = pl.pallas_call(
        functools.partial(kernel, rows, cols, inline_count, xline_count),
        out_shape=jax.ShapeDtypeStruct((own, samples), F32),
        in_specs=[pl.BlockSpec(memory_space=pltpu.HBM)] * len(operands),
        out_specs=pl.BlockSpec(memory_space=pltpu.VMEM),
        scratch_shapes=[
            pltpu.VMEM((own, samples), F32),
            pltpu.VMEM((own, lanes), F32),
            pltpu.VMEM((GROUPS, own, lanes), BF16),
            pltpu.VMEM((GROUPS, own, lanes), BF16),
            pltpu.VMEM((GROUPS, 2, rows * HALF, lanes), F32),
            pltpu.VMEM((GROUPS, rows * (cols - 2 * HALF), lanes), F32),
            pltpu.VMEM((GROUPS, around, lanes), F32),
            pltpu.VMEM((GROUPS, waves, lanes), F32),
            pltpu.VMEM((GROUPS, waves, lanes), F32),
            pltpu.VMEM((2, waves, lanes), BF16),
            pltpu.VMEM((2, TAP_ROWS, frequencies), F32),
            pltpu.VMEM((tap_count, 2, frequencies), F32),
            pltpu.VMEM(forward.shape, BF16),
            pltpu.VMEM(inverse.shape, BF16),
            pltpu.VMEM(first.shape, BF16),
            pltpu.VMEM(second.shape[1:], BF16),
            pltpu.VMEM(taps.shape, BF16),
            pltpu.VMEM(back.shape, BF16),
            pltpu.VMEM(order.shape, BF16),
            pltpu.SemaphoreType.DMA((8 + GROUPS,)),
            pltpu.SemaphoreType.DMA((copies,)),
            pltpu.SemaphoreType.DMA((copies,)),
        ],
        compiler_params=pltpu.CompilerParams(
            collective_id=0, has_side_effects=True, vmem_limit_bytes=60 * 1024 * 1024
        ),
    )(*operands)
    result = pl.pallas_call(
        functools.partial(pass_on, own),
        out_shape=jax.ShapeDtypeStruct((own, samples), F32),
        in_specs=[pl.BlockSpec(memory_space=pltpu.HBM)],
        out_specs=pl.BlockSpec(memory_space=pltpu.HBM),
        scratch_shapes=[pltpu.SemaphoreType.DMA((PIECES,))],
        compiler_params=pltpu.CompilerParams(vmem_limit_bytes=60 * 1024 * 1024),
    )(result)
    return result.reshape(rows, cols, samples)


def solution(mesh):
    return jax.shard_map(
        functools.partial(
            per_device, inline_count=mesh.shape["inline"], xline_count=mesh.shape["xline"]
        ),
        mesh=mesh,
        in_specs=(P("inline", "xline", None), P()),
        out_specs=P("inline", "xline", None),
        check_vma=False,
    )
```

```python
import functools

import jax
import jax.numpy as jnp
import ml_dtypes
import numpy as np
from jax import lax
from jax.experimental import pallas as pl
from jax.experimental.pallas import tpu as pltpu
from jax.sharding import PartitionSpec as P

HALF = 4
GROUPS = 2
TAP_ROWS = 96
MESH = pl.DeviceIdType.MESH
BF16 = jnp.bfloat16
F32 = jnp.float32


def halves(table):
    high = table.astype(np.float32).astype(ml_dtypes.bfloat16)
    low = (table - high.astype(np.float64)).astype(np.float32).astype(ml_dtypes.bfloat16)
    return np.stack((high, low))


def bin_groups(frequencies):
    order = np.concatenate((np.arange(0, frequencies, 2), np.arange(1, frequencies, 2)))
    return order.reshape(GROUPS, frequencies // GROUPS)


def temporal_tables(samples, frequencies):
    time = np.arange(samples // 2)[:, None]
    forward, inverse = [], []
    for bins in bin_groups(frequencies):
        angle = 2.0 * np.pi * (time * bins[None, :] % samples) / samples
        weight = np.where(bins == 0, 1.0, 2.0)[None, :] / samples
        forward.append(np.concatenate((np.cos(angle), -np.sin(angle)), axis=1))
        inverse.append(np.concatenate((weight * np.cos(angle), -weight * np.sin(angle)), axis=1).T)
    return halves(np.stack(forward)), halves(np.stack(inverse))


def spatial_frequencies(height, width):
    chosen = []
    for row in range(height):
        for col in range(width):
            mirror = ((height - row) % height, (width - col) % width)
            if (row, col) <= mirror:
                chosen.append((row, col, 1.0 if (row, col) == mirror else 2.0))
    return np.array(chosen)


def spatial_basis(waves, padded, height, width, positions):
    positions = np.asarray(positions)
    turns = np.outer(waves[:, 0], positions[:, 0]) / height + np.outer(waves[:, 1], positions[:, 1]) / width
    angle = 2.0 * np.pi * turns
    basis = np.zeros((2 * padded, len(positions)))
    basis[: len(waves)] = np.cos(angle)
    basis[padded : padded + len(waves)] = np.sin(angle)
    return basis


def grid(rows, cols):
    return [(row, col) for row in rows for col in cols]


def stacked(table):
    both = halves(table)
    return np.concatenate((both[0], both[1]), axis=0)


def thrice(table):
    both = halves(table)
    return np.concatenate((both[0], both[0], both[1]), axis=1)


def layout(rows, cols, sides):
    strip, ends, middle = rows * HALF, HALF * HALF, HALF * (cols - 2 * HALF)
    sizes = [("left", strip), ("right", strip)]
    for side in range(sides):
        sizes += [(("low", side), ends), (("high", side), ends), (("middle", side), middle)]
        sizes += [(("from_left", side), ends), (("from_right", side), ends)]
    places, at = {}, 0
    for name, size in sizes:
        places[name] = (at, size)
        at += size
    return places, at


def spatial_tables(rows, cols, inline_count):
    height, width = rows + 2 * HALF, cols + 2 * HALF
    waves = spatial_frequencies(height, width)
    padded = -(-len(waves) // 16) * 16
    basis = functools.partial(spatial_basis, waves, padded, height, width)
    below_zero, above_end = range(-HALF, 0), range(cols, cols + HALF)
    own = grid(range(rows), range(cols))
    above, below = range(-HALF, 0), range(rows, rows + HALF)
    variants = [[below], [above]] if inline_count == 2 else [[above, below]]
    sides = min(inline_count - 1, 2)
    second = []
    for bands in variants:
        places = grid(range(rows), below_zero) + grid(range(rows), above_end)
        for band in bands[:sides]:
            places += grid(band, range(HALF)) + grid(band, range(cols - HALF, cols))
            places += grid(band, range(HALF, cols - HALF))
            places += grid(band, below_zero) + grid(band, above_end)
        second.append(thrice(basis(places)))
    reach = range(-HALF, HALF + 1)
    taps = np.zeros((2 * padded, TAP_ROWS))
    taps[:, : len(reach) ** 2] = basis(grid(reach, reach))
    count = np.zeros((2 * padded, 1))
    count[: len(waves), 0] = waves[:, 2] / (height * width)
    count[padded : padded + len(waves), 0] = -waves[:, 2] / (height * width)
    back = (count * basis(own)).T
    return thrice(basis(own)), np.stack(second), thrice(taps), stacked(back)


def parts(value):
    high = value.astype(BF16)
    return high, (value - high.astype(F32)).astype(BF16)


def product(left, high, low):
    dot = functools.partial(jnp.dot, preferred_element_type=F32)
    count = left.shape[0] // 2
    both = dot(left, high)
    return both[:count] + (both[count:] + dot(left[:count], low))


def summed(left, high, low):
    return jnp.dot(left, jnp.concatenate((high, low, high), axis=0), preferred_element_type=F32)


def kernel(
    rows, cols, inline_count, xline_count,
    traces, filters, temporal, spatial,
    out,
    own_in, own, own_high, own_low, ends, middle, halo, wave, response, kept, tap_rows,
    filters_in, forward_in, inverse_in, first_in, second_in, taps_in, back_in, order_in,
    local_sem, send_sem, recv_sem,
):
    sides = min(inline_count - 1, 2)
    places, _ = layout(rows, cols, sides)
    fold = own_in.shape[1] // 2
    lanes = wave.shape[2]
    bins = lanes // 2
    padded = wave.shape[1] // 2
    inner = cols - 2 * HALF

    me_i = lax.axis_index("inline")
    me_x = lax.axis_index("xline")

    has_left, has_right = me_x > 0, me_x < xline_count - 1
    at_left, at_right = {"xline": me_x - 1}, {"xline": me_x + 1}
    if inline_count == 2:
        bands = [(None, {"inline": 1 - me_i}, (1 - me_i) * (rows - HALF), 0)]
        present = [None]
    elif inline_count > 2:
        has_above, has_below = me_i > 0, me_i < inline_count - 1
        bands = [
            (has_above, {"inline": me_i - 1}, 0, 1),
            (has_below, {"inline": me_i + 1}, rows - HALF, 0),
        ]
        present = [has_above, has_below]
    else:
        bands, present = [], []

    def when(condition, action):
        if condition is None:
            action()
        else:
            pl.when(condition)(action)

    barrier = pltpu.get_barrier_semaphore()
    neighbours = [(has_left, at_left), (has_right, at_right)]
    neighbours += [(exists, where) for exists, where, _, _ in bands]
    for exists, where in neighbours:
        when(exists, lambda: pl.semaphore_signal(barrier, inc=1, device_id=where, device_id_type=MESH))

    def load(source, target, slot):
        return pltpu.make_async_copy(source, target, local_sem.at[slot])

    load_own = load(traces, own_in, 0)
    load_forward = [load(temporal.at[0, :, group], forward_in.at[:, group], 1 + group) for group in range(GROUPS)]
    waves = wave.shape[1]

    def table(start, target, slot):
        count = target.shape[0]
        return load(spatial.at[pl.ds(start, count)], target, slot)

    base = 1 + GROUPS
    load_filters = load(filters, filters_in, base)
    frequencies = order_in.shape[0]
    load_order = table(0, order_in, base + 1)
    load_taps = table(frequencies, taps_in, base + 2)
    load_first = table(frequencies + waves, first_in, base + 3)
    after = frequencies + 2 * waves
    load_back = table(after, back_in, base + 5)
    after += back_in.shape[0]
    if inline_count == 2:
        after = pl.multiple_of(after + me_i * waves, 16)
    load_second = table(after, second_in, base + 4)
    load_inverse = load(temporal.at[1], inverse_in, base + 6)
    loads = [load_own, *load_forward, load_filters, load_order, load_taps]
    loads += [load_first, load_second, load_back, load_inverse]
    for each in loads:
        each.start()

    def clear(*names):
        for name in names:
            at, size = places[name]
            halo[:, at : at + size, :] = jnp.zeros((GROUPS, size, lanes), F32)

    pl.when(jnp.logical_not(has_left))(lambda: clear("left", *[("from_left", s) for s in range(sides)]))
    pl.when(jnp.logical_not(has_right))(lambda: clear("right", *[("from_right", s) for s in range(sides)]))
    for side, exists in enumerate(present):
        if exists is not None:
            pieces = [(kind, side) for kind in ("low", "high", "middle", "from_left", "from_right")]
            pl.when(jnp.logical_not(exists))(lambda: clear(*pieces))

    slots = {name: slot for slot, name in enumerate(places)}

    def remote(group, name, source, where):
        at, size = places[name]
        slot = group * len(places) + slots[name]
        return pltpu.make_async_remote_copy(
            src_ref=source,
            dst_ref=halo.at[group, pl.ds(at, size)],
            send_sem=send_sem.at[slot],
            recv_sem=recv_sem.at[slot],
            device_id=where,
            device_id_type=MESH,
        )

    def landed(group, name):
        at, size = places[name]
        return halo.at[group, pl.ds(at, size)]

    def come(group, name):
        remote(group, name, landed(group, name), at_left).wait_recv()

    sent = []

    def send(condition, copy):
        when(condition, copy.start)
        sent.append((condition, copy))

    load_own.wait()
    for group in range(GROUPS):
        if group % (GROUPS // 2) == 0:
            if group == 0:
                folded = own_in[:, :fold] + own_in[:, fold:]
            else:
                folded = own_in[:, :fold] - own_in[:, fold:]
            folded = jnp.concatenate(parts(folded), axis=0)
        load_forward[group].wait()
        spectrum = product(folded, forward_in[0, group], forward_in[1, group])
        own[...] = spectrum
        high, low = parts(spectrum)
        own_high[group] = high
        own_low[group] = low
        for row in range(rows):
            at = row * cols
            ends[group, 0, row * HALF : (row + 1) * HALF, :] = own[at : at + HALF, :]
            ends[group, 1, row * HALF : (row + 1) * HALF, :] = own[at + cols - HALF : at + cols, :]
            middle[group, row * inner : (row + 1) * inner, :] = own[at + HALF : at + cols - HALF, :]
        if group == 0:
            peers = sum(1 if exists is None else exists.astype(jnp.int32) for exists, _ in neighbours)
            pl.semaphore_wait(barrier, peers)
        for exists, where, start, side in bands:
            few = pl.ds(pl.multiple_of(start * HALF, HALF * HALF), HALF * HALF)
            send(exists, remote(group, ("low", side), ends.at[group, 0, few], where))
            send(exists, remote(group, ("high", side), ends.at[group, 1, few], where))
        send(has_left, remote(group, "right", ends.at[group, 0], at_left))
        send(has_right, remote(group, "left", ends.at[group, 1], at_right))
    for group in range(GROUPS):
        for exists, where, start, side in bands:
            many = pl.ds(pl.multiple_of(start * inner, HALF * inner), HALF * inner)
            send(exists, remote(group, ("middle", side), middle.at[group, many], where))

    def forward_ends(group):
        for side, exists in enumerate(present):
            def on(side=side):
                come(group, ("low", side))
                come(group, ("high", side))
                to_left = remote(group, ("from_right", side), landed(group, ("low", side)), at_left)
                to_right = remote(group, ("from_left", side), landed(group, ("high", side)), at_right)
                pl.when(has_left)(to_left.start)
                pl.when(has_right)(to_right.start)

            when(exists, on)

    def sent_ends(group):
        for side, exists in enumerate(present):
            def on(side=side):
                to_left = remote(group, ("from_right", side), landed(group, ("low", side)), at_left)
                to_right = remote(group, ("from_left", side), landed(group, ("high", side)), at_right)
                pl.when(has_left)(to_left.wait_send)
                pl.when(has_right)(to_right.wait_send)

            when(exists, on)

    forward_ends(0)
    load_filters.wait()
    load_order.wait()
    load_taps.wait()
    tap_count = filters_in.shape[0]
    tap_rows[...] = jnp.zeros_like(tap_rows)
    for part in range(2):
        tap_rows[part, :tap_count, :] = filters_in[:, part, :]
    real, imag = parts(tap_rows[0]), parts(tap_rows[1])
    ordered = jnp.dot(
        jnp.concatenate((real[0], imag[0], real[1], imag[1]), axis=0),
        order_in[:, :frequencies],
        preferred_element_type=F32
    ).astype(BF16)
    for group in range(GROUPS):
        mine = slice(group * bins, (group + 1) * bins)
        pieces = [ordered[TAP_ROWS * piece : TAP_ROWS * (piece + 1), mine] for piece in range(4)]
        response[group] = summed(
            taps_in[:, : 3 * TAP_ROWS], jnp.concatenate(pieces[:2], axis=1), jnp.concatenate(pieces[2:], axis=1)
        )
    load_first.wait()
    for group in range(GROUPS):
        wave[group] = summed(first_in[:, : 3 * rows * cols], own_high[group], own_low[group])
        if group == 0:
            forward_ends(GROUPS - 1)

    load_second.wait()
    load_back.wait()
    load_inverse.wait()
    halfway = [None, None]
    for group in range(GROUPS):
        pl.when(has_left)(lambda: come(group, "left"))
        pl.when(has_right)(lambda: come(group, "right"))
        for side, exists in enumerate(present):
            def rest(side=side):
                come(group, ("middle", side))
                pl.when(has_left)(lambda: come(group, ("from_left", side)))
                pl.when(has_right)(lambda: come(group, ("from_right", side)))

            when(exists, rest)
        high, low = parts(halo[group])
        wave[group] += summed(second_in[:, : 3 * halo.shape[1]], high, low)

        rc, rs = wave[group, :padded, :bins], wave[group, padded:, :bins]
        ic, js = wave[group, :padded, bins:], wave[group, padded:, bins:]
        frc, frs = response[group, :padded, :bins], response[group, padded:, :bins]
        fic, fis = response[group, :padded, bins:], response[group, padded:, bins:]
        outcome = {
            (0, 0): rc * frc + rs * frs - (ic * fic + js * fis),
            (1, 0): rc * frs - rs * frc - (ic * fis - js * fic),
            (0, 1): rc * fic + rs * fis + (ic * frc + js * frs),
            (1, 1): rc * fis - rs * fic + (ic * frs - js * frc),
        }
        for (which, part), value in outcome.items():
            high, low = parts(value)
            kept[0, which * padded : (which + 1) * padded, part * bins : (part + 1) * bins] = high
            kept[1, which * padded : (which + 1) * padded, part * bins : (part + 1) * bins] = low
        filtered = product(back_in[:, : 2 * padded], kept[0], kept[1])
        filtered = jnp.concatenate(parts(filtered), axis=0)
        piece = product(filtered, inverse_in[0, group], inverse_in[1, group])
        parity = group // (GROUPS // 2)
        halfway[parity] = piece if halfway[parity] is None else halfway[parity] + piece
    out[:, :fold] = halfway[0] + halfway[1]
    out[:, fold:] = halfway[0] - halfway[1]

    for condition, copy in sent:
        when(condition, copy.wait_send)
    for group in range(GROUPS):
        sent_ends(group)


def per_device(traces, filters, inline_count, xline_count):
    rows, cols, samples = traces.shape
    _, frequencies, tap_count = filters.shape
    forward, inverse = temporal_tables(samples, frequencies)
    first, second, taps, back = spatial_tables(rows, cols, inline_count)
    order = np.zeros((frequencies, frequencies), ml_dtypes.bfloat16)
    order[bin_groups(frequencies).reshape(-1), np.arange(frequencies)] = 1.0
    sides = min(inline_count - 1, 2)
    places, around = layout(rows, cols, sides)
    own = rows * cols
    waves = first.shape[0]
    lanes = 2 * frequencies // GROUPS
    pieces = [order, taps, first, back, *second]
    wide = -(-max(piece.shape[1] for piece in pieces) // 128) * 128
    spatial = np.concatenate([np.pad(piece, ((0, 0), (0, wide - piece.shape[1]))) for piece in pieces])
    operands = [traces.reshape(own, samples), filters.transpose(2, 0, 1)]
    operands += [jnp.asarray(np.stack((forward, inverse))), jnp.asarray(spatial)]
    copies = GROUPS * len(places)
    result = pl.pallas_call(
        functools.partial(kernel, rows, cols, inline_count, xline_count),
        out_shape=jax.ShapeDtypeStruct((own, samples), F32),
        in_specs=[pl.BlockSpec(memory_space=pltpu.HBM)] * len(operands),
        out_specs=pl.BlockSpec(memory_space=pltpu.VMEM),
        scratch_shapes=[
            pltpu.VMEM((own, samples), F32),
            pltpu.VMEM((own, lanes), F32),
            pltpu.VMEM((GROUPS, own, lanes), BF16),
            pltpu.VMEM((GROUPS, own, lanes), BF16),
            pltpu.VMEM((GROUPS, 2, rows * HALF, lanes), F32),
            pltpu.VMEM((GROUPS, rows * (cols - 2 * HALF), lanes), F32),
            pltpu.VMEM((GROUPS, around, lanes), F32),
            pltpu.VMEM((GROUPS, waves, lanes), F32),
            pltpu.VMEM((GROUPS, waves, lanes), F32),
            pltpu.VMEM((2, waves, lanes), BF16),
            pltpu.VMEM((2, TAP_ROWS, frequencies), F32),
            pltpu.VMEM((tap_count, 2, frequencies), F32),
            pltpu.VMEM(forward.shape, BF16),
            pltpu.VMEM(inverse.shape, BF16),
            pltpu.VMEM((waves, wide), BF16),
            pltpu.VMEM((waves, wide), BF16),
            pltpu.VMEM((waves, wide), BF16),
            pltpu.VMEM((back.shape[0], wide), BF16),
            pltpu.VMEM((frequencies, wide), BF16),
            pltpu.SemaphoreType.DMA((8 + GROUPS,)),
            pltpu.SemaphoreType.DMA((copies,)),
            pltpu.SemaphoreType.DMA((copies,)),
        ],
        compiler_params=pltpu.CompilerParams(
            collective_id=0, has_side_effects=True, vmem_limit_bytes=53 * 1024 * 1024
        ),
    )(*operands)
    return result.reshape(rows, cols, samples)


def solution(mesh):
    return jax.shard_map(
        functools.partial(
            per_device, inline_count=mesh.shape["inline"], xline_count=mesh.shape["xline"]
        ),
        mesh=mesh,
        in_specs=(P("inline", "xline", None), P()),
        out_specs=P("inline", "xline", None),
        check_vma=False,
    )
```

```python
import functools

import jax
import jax.numpy as jnp
import ml_dtypes
import numpy as np
from jax import lax
from jax.experimental import pallas as pl
from jax.experimental.pallas import tpu as pltpu
from jax.sharding import PartitionSpec as P

HALF = 4
GROUPS = 2
TAP_ROWS = 96
MESH = pl.DeviceIdType.MESH
BF16 = jnp.bfloat16
F32 = jnp.float32


def halves(table):
    high = table.astype(np.float32).astype(ml_dtypes.bfloat16)
    low = (table - high.astype(np.float64)).astype(np.float32).astype(ml_dtypes.bfloat16)
    return np.stack((high, low))


def bin_groups(frequencies):
    order = np.concatenate((np.arange(0, frequencies, 2), np.arange(1, frequencies, 2)))
    return order.reshape(GROUPS, frequencies // GROUPS)


def temporal_tables(samples, frequencies):
    time = np.arange(samples // 2)[:, None]
    forward, inverse = [], []
    for bins in bin_groups(frequencies):
        angle = 2.0 * np.pi * (time * bins[None, :] % samples) / samples
        weight = np.where(bins == 0, 1.0, 2.0)[None, :] / samples
        forward.append(np.concatenate((np.cos(angle), -np.sin(angle)), axis=1))
        inverse.append(np.concatenate((weight * np.cos(angle), -weight * np.sin(angle)), axis=1).T)
    return halves(np.stack(forward)), halves(np.stack(inverse))


def spatial_frequencies(height, width):
    chosen = []
    for row in range(height):
        for col in range(width):
            mirror = ((height - row) % height, (width - col) % width)
            if (row, col) <= mirror:
                chosen.append((row, col, 1.0 if (row, col) == mirror else 2.0))
    return np.array(chosen)


def spatial_basis(waves, padded, height, width, positions):
    positions = np.asarray(positions)
    turns = np.outer(waves[:, 0], positions[:, 0]) / height + np.outer(waves[:, 1], positions[:, 1]) / width
    angle = 2.0 * np.pi * turns
    basis = np.zeros((2 * padded, len(positions)))
    basis[: len(waves)] = np.cos(angle)
    basis[padded : padded + len(waves)] = np.sin(angle)
    return basis


def grid(rows, cols):
    return [(row, col) for row in rows for col in cols]


def stacked(table):
    both = halves(table)
    return np.concatenate((both[0], both[1]), axis=0)


def thrice(table):
    both = halves(table)
    return np.concatenate((both[0], both[0], both[1]), axis=1)


def layout(rows, cols, sides):
    strip, ends, middle = rows * HALF, HALF * HALF, HALF * (cols - 2 * HALF)
    sizes = [("left", strip), ("right", strip)]
    for side in range(sides):
        sizes += [(("low", side), ends), (("high", side), ends), (("middle", side), middle)]
        sizes += [(("from_left", side), ends), (("from_right", side), ends)]
    places, at = {}, 0
    for name, size in sizes:
        places[name] = (at, size)
        at += size
    return places, at


def spatial_tables(rows, cols, inline_count):
    height, width = rows + 2 * HALF, cols + 2 * HALF
    waves = spatial_frequencies(height, width)
    padded = -(-len(waves) // 16) * 16
    basis = functools.partial(spatial_basis, waves, padded, height, width)
    below_zero, above_end = range(-HALF, 0), range(cols, cols + HALF)
    own = grid(range(rows), range(cols))
    above, below = range(-HALF, 0), range(rows, rows + HALF)
    variants = [[below], [above]] if inline_count == 2 else [[above, below]]
    sides = min(inline_count - 1, 2)
    second = []
    for bands in variants:
        places = grid(range(rows), below_zero) + grid(range(rows), above_end)
        for band in bands[:sides]:
            places += grid(band, range(HALF)) + grid(band, range(cols - HALF, cols))
            places += grid(band, range(HALF, cols - HALF))
            places += grid(band, below_zero) + grid(band, above_end)
        second.append(thrice(basis(places)))
    reach = range(-HALF, HALF + 1)
    taps = np.zeros((2 * padded, TAP_ROWS))
    taps[:, : len(reach) ** 2] = basis(grid(reach, reach))
    count = np.zeros((2 * padded, 1))
    count[: len(waves), 0] = waves[:, 2] / (height * width)
    count[padded : padded + len(waves), 0] = -waves[:, 2] / (height * width)
    back = (count * basis(own)).T
    return thrice(basis(own)), np.stack(second), thrice(taps), stacked(back)


def parts(value):
    high = value.astype(BF16)
    return high, (value - high.astype(F32)).astype(BF16)


def product(left, high, low):
    dot = functools.partial(jnp.dot, preferred_element_type=F32)
    count = left.shape[0] // 2
    both = dot(left, high)
    return both[:count] + (both[count:] + dot(left[:count], low))


def summed(left, high, low):
    return jnp.dot(left, jnp.concatenate((high, low, high), axis=0), preferred_element_type=F32)


def kernel(
    rows, cols, inline_count, xline_count,
    traces, filters, temporal, spatial,
    out,
    own_in, own, own_high, own_low, ends, middle, halo, wave, response, kept, tap_rows,
    filters_in, forward_in, inverse_in, first_in, second_in, taps_in, back_in, order_in,
    local_sem, send_sem, recv_sem,
):
    sides = min(inline_count - 1, 2)
    places, _ = layout(rows, cols, sides)
    fold = own_in.shape[1] // 2
    lanes = wave.shape[2]
    bins = lanes // 2
    padded = wave.shape[1] // 2
    inner = cols - 2 * HALF

    me_i = lax.axis_index("inline")
    me_x = lax.axis_index("xline")

    has_left, has_right = me_x > 0, me_x < xline_count - 1
    at_left, at_right = {"xline": me_x - 1}, {"xline": me_x + 1}
    if inline_count == 2:
        bands = [(None, {"inline": 1 - me_i}, (1 - me_i) * (rows - HALF), 0)]
        present = [None]
    elif inline_count > 2:
        has_above, has_below = me_i > 0, me_i < inline_count - 1
        bands = [
            (has_above, {"inline": me_i - 1}, 0, 1),
            (has_below, {"inline": me_i + 1}, rows - HALF, 0),
        ]
        present = [has_above, has_below]
    else:
        bands, present = [], []

    def when(condition, action):
        if condition is None:
            action()
        else:
            pl.when(condition)(action)

    barrier = pltpu.get_barrier_semaphore()
    neighbours = [(has_left, at_left), (has_right, at_right)]
    neighbours += [(exists, where) for exists, where, _, _ in bands]
    for exists, where in neighbours:
        when(exists, lambda: pl.semaphore_signal(barrier, inc=1, device_id=where, device_id_type=MESH))

    def load(source, target, slot):
        return pltpu.make_async_copy(source, target, local_sem.at[slot])

    load_own = load(traces, own_in, 0)
    load_forward = [load(temporal.at[0, :, group], forward_in.at[:, group], 1 + group) for group in range(GROUPS)]
    waves = wave.shape[1]

    def table(start, target, slot):
        count = target.shape[0]
        return load(spatial.at[pl.ds(start, count)], target, slot)

    base = 1 + GROUPS
    load_filters = load(filters, filters_in, base)
    frequencies = order_in.shape[0]
    load_order = table(0, order_in, base + 1)
    load_taps = table(frequencies, taps_in, base + 2)
    load_first = table(frequencies + waves, first_in, base + 3)
    after = frequencies + 2 * waves
    load_back = table(after, back_in, base + 5)
    after += back_in.shape[0]
    if inline_count == 2:
        after = pl.multiple_of(after + me_i * waves, 16)
    load_second = table(after, second_in, base + 4)
    load_inverse = load(temporal.at[1], inverse_in, base + 6)
    loads = [load_own, *load_forward, load_filters, load_order, load_taps]
    loads += [load_first, load_second, load_back, load_inverse]
    for each in loads:
        each.start()

    def clear(*names):
        for name in names:
            at, size = places[name]
            halo[:, at : at + size, :] = jnp.zeros((GROUPS, size, lanes), F32)

    pl.when(jnp.logical_not(has_left))(lambda: clear("left", *[("from_left", s) for s in range(sides)]))
    pl.when(jnp.logical_not(has_right))(lambda: clear("right", *[("from_right", s) for s in range(sides)]))
    for side, exists in enumerate(present):
        if exists is not None:
            pieces = [(kind, side) for kind in ("low", "high", "middle", "from_left", "from_right")]
            pl.when(jnp.logical_not(exists))(lambda: clear(*pieces))

    slots = {name: slot for slot, name in enumerate(places)}

    def remote(group, name, source, where):
        at, size = places[name]
        slot = group * len(places) + slots[name]
        return pltpu.make_async_remote_copy(
            src_ref=source,
            dst_ref=halo.at[group, pl.ds(at, size)],
            send_sem=send_sem.at[slot],
            recv_sem=recv_sem.at[slot],
            device_id=where,
            device_id_type=MESH,
        )

    def landed(group, name):
        at, size = places[name]
        return halo.at[group, pl.ds(at, size)]

    def come(group, name):
        remote(group, name, landed(group, name), at_left).wait_recv()

    sent = []

    def send(condition, copy):
        when(condition, copy.start)
        sent.append((condition, copy))

    load_own.wait()
    for group in range(GROUPS):
        if group % (GROUPS // 2) == 0:
            if group == 0:
                folded = own_in[:, :fold] + own_in[:, fold:]
            else:
                folded = own_in[:, :fold] - own_in[:, fold:]
            folded = jnp.concatenate(parts(folded), axis=0)
        load_forward[group].wait()
        spectrum = product(folded, forward_in[0, group], forward_in[1, group])
        own[...] = spectrum
        high, low = parts(spectrum)
        own_high[group] = high
        own_low[group] = low
        for row in range(rows):
            at = row * cols
            ends[group, 0, row * HALF : (row + 1) * HALF, :] = own[at : at + HALF, :]
            ends[group, 1, row * HALF : (row + 1) * HALF, :] = own[at + cols - HALF : at + cols, :]
            middle[group, row * inner : (row + 1) * inner, :] = own[at + HALF : at + cols - HALF, :]
        if group == 0:
            peers = sum(1 if exists is None else exists.astype(jnp.int32) for exists, _ in neighbours)
            pl.semaphore_wait(barrier, peers)
        for exists, where, start, side in bands:
            few = pl.ds(pl.multiple_of(start * HALF, HALF * HALF), HALF * HALF)
            send(exists, remote(group, ("low", side), ends.at[group, 0, few], where))
            send(exists, remote(group, ("high", side), ends.at[group, 1, few], where))
        send(has_left, remote(group, "right", ends.at[group, 0], at_left))
        send(has_right, remote(group, "left", ends.at[group, 1], at_right))
    for group in range(GROUPS):
        for exists, where, start, side in bands:
            many = pl.ds(pl.multiple_of(start * inner, HALF * inner), HALF * inner)
            send(exists, remote(group, ("middle", side), middle.at[group, many], where))

    def forward_ends(group):
        for side, exists in enumerate(present):
            def on(side=side):
                come(group, ("low", side))
                come(group, ("high", side))
                to_left = remote(group, ("from_right", side), landed(group, ("low", side)), at_left)
                to_right = remote(group, ("from_left", side), landed(group, ("high", side)), at_right)
                pl.when(has_left)(to_left.start)
                pl.when(has_right)(to_right.start)

            when(exists, on)

    def sent_ends(group):
        for side, exists in enumerate(present):
            def on(side=side):
                to_left = remote(group, ("from_right", side), landed(group, ("low", side)), at_left)
                to_right = remote(group, ("from_left", side), landed(group, ("high", side)), at_right)
                pl.when(has_left)(to_left.wait_send)
                pl.when(has_right)(to_right.wait_send)

            when(exists, on)

    forward_ends(0)
    load_filters.wait()
    load_order.wait()
    load_taps.wait()
    tap_count = filters_in.shape[0]
    tap_rows[...] = jnp.zeros_like(tap_rows)
    for part in range(2):
        tap_rows[part, :tap_count, :] = filters_in[:, part, :]
    real, imag = parts(tap_rows[0]), parts(tap_rows[1])
    ordered = jnp.dot(
        jnp.concatenate((real[0], imag[0], real[1], imag[1]), axis=0),
        order_in[:, :frequencies],
        preferred_element_type=F32
    ).astype(BF16)
    for group in range(GROUPS):
        mine = slice(group * bins, (group + 1) * bins)
        pieces = [ordered[TAP_ROWS * piece : TAP_ROWS * (piece + 1), mine] for piece in range(4)]
        response[group] = summed(
            taps_in[:, : 3 * TAP_ROWS], jnp.concatenate(pieces[:2], axis=1), jnp.concatenate(pieces[2:], axis=1)
        )
        if group < GROUPS - 1:
            forward_ends(group + 1)
    load_first.wait()
    for group in range(GROUPS):
        wave[group] = summed(first_in[:, : 3 * rows * cols], own_high[group], own_low[group])

    load_second.wait()
    load_back.wait()
    load_inverse.wait()
    halfway = [None, None]
    for group in range(GROUPS):
        pl.when(has_left)(lambda: come(group, "left"))
        pl.when(has_right)(lambda: come(group, "right"))
        for side, exists in enumerate(present):
            def rest(side=side):
                come(group, ("middle", side))
                pl.when(has_left)(lambda: come(group, ("from_left", side)))
                pl.when(has_right)(lambda: come(group, ("from_right", side)))

            when(exists, rest)
        high, low = parts(halo[group])
        wave[group] += summed(second_in[:, : 3 * halo.shape[1]], high, low)

        rc, rs = wave[group, :padded, :bins], wave[group, padded:, :bins]
        ic, js = wave[group, :padded, bins:], wave[group, padded:, bins:]
        frc, frs = response[group, :padded, :bins], response[group, padded:, :bins]
        fic, fis = response[group, :padded, bins:], response[group, padded:, bins:]
        outcome = {
            (0, 0): rc * frc + rs * frs - (ic * fic + js * fis),
            (1, 0): rc * frs - rs * frc - (ic * fis - js * fic),
            (0, 1): rc * fic + rs * fis + (ic * frc + js * frs),
            (1, 1): rc * fis - rs * fic + (ic * frs - js * frc),
        }
        for (which, part), value in outcome.items():
            high, low = parts(value)
            kept[0, which * padded : (which + 1) * padded, part * bins : (part + 1) * bins] = high
            kept[1, which * padded : (which + 1) * padded, part * bins : (part + 1) * bins] = low
        filtered = product(back_in[:, : 2 * padded], kept[0], kept[1])
        filtered = jnp.concatenate(parts(filtered), axis=0)
        piece = product(filtered, inverse_in[0, group], inverse_in[1, group])
        parity = group // (GROUPS // 2)
        halfway[parity] = piece if halfway[parity] is None else halfway[parity] + piece
    out[:, :fold] = halfway[0] + halfway[1]
    out[:, fold:] = halfway[0] - halfway[1]

    for condition, copy in sent:
        when(condition, copy.wait_send)
    for group in range(GROUPS):
        sent_ends(group)


def per_device(traces, filters, inline_count, xline_count):
    rows, cols, samples = traces.shape
    _, frequencies, tap_count = filters.shape
    forward, inverse = temporal_tables(samples, frequencies)
    first, second, taps, back = spatial_tables(rows, cols, inline_count)
    order = np.zeros((frequencies, frequencies), ml_dtypes.bfloat16)
    order[bin_groups(frequencies).reshape(-1), np.arange(frequencies)] = 1.0
    sides = min(inline_count - 1, 2)
    places, around = layout(rows, cols, sides)
    own = rows * cols
    waves = first.shape[0]
    lanes = 2 * frequencies // GROUPS
    pieces = [order, taps, first, back, *second]
    wide = -(-max(piece.shape[1] for piece in pieces) // 128) * 128
    spatial = np.concatenate([np.pad(piece, ((0, 0), (0, wide - piece.shape[1]))) for piece in pieces])
    operands = [traces.reshape(own, samples), filters.transpose(2, 0, 1)]
    operands += [jnp.asarray(np.stack((forward, inverse))), jnp.asarray(spatial)]
    copies = GROUPS * len(places)
    result = pl.pallas_call(
        functools.partial(kernel, rows, cols, inline_count, xline_count),
        out_shape=jax.ShapeDtypeStruct((own, samples), F32),
        in_specs=[pl.BlockSpec(memory_space=pltpu.HBM)] * len(operands),
        out_specs=pl.BlockSpec(memory_space=pltpu.VMEM),
        scratch_shapes=[
            pltpu.VMEM((own, samples), F32),
            pltpu.VMEM((own, lanes), F32),
            pltpu.VMEM((GROUPS, own, lanes), BF16),
            pltpu.VMEM((GROUPS, own, lanes), BF16),
            pltpu.VMEM((GROUPS, 2, rows * HALF, lanes), F32),
            pltpu.VMEM((GROUPS, rows * (cols - 2 * HALF), lanes), F32),
            pltpu.VMEM((GROUPS, around, lanes), F32),
            pltpu.VMEM((GROUPS, waves, lanes), F32),
            pltpu.VMEM((GROUPS, waves, lanes), F32),
            pltpu.VMEM((2, waves, lanes), BF16),
            pltpu.VMEM((2, TAP_ROWS, frequencies), F32),
            pltpu.VMEM((tap_count, 2, frequencies), F32),
            pltpu.VMEM(forward.shape, BF16),
            pltpu.VMEM(inverse.shape, BF16),
            pltpu.VMEM((waves, wide), BF16),
            pltpu.VMEM((waves, wide), BF16),
            pltpu.VMEM((waves, wide), BF16),
            pltpu.VMEM((back.shape[0], wide), BF16),
            pltpu.VMEM((frequencies, wide), BF16),
            pltpu.SemaphoreType.DMA((8 + GROUPS,)),
            pltpu.SemaphoreType.DMA((copies,)),
            pltpu.SemaphoreType.DMA((copies,)),
        ],
        compiler_params=pltpu.CompilerParams(
            collective_id=0, has_side_effects=True, vmem_limit_bytes=53 * 1024 * 1024
        ),
    )(*operands)
    return result.reshape(rows, cols, samples)


def solution(mesh):
    return jax.shard_map(
        functools.partial(
            per_device, inline_count=mesh.shape["inline"], xline_count=mesh.shape["xline"]
        ),
        mesh=mesh,
        in_specs=(P("inline", "xline", None), P()),
        out_specs=P("inline", "xline", None),
        check_vma=False,
    )
```

```python
import functools

import jax
import jax.numpy as jnp
import ml_dtypes
import numpy as np
from jax import lax
from jax.experimental import pallas as pl
from jax.experimental.pallas import tpu as pltpu
from jax.sharding import PartitionSpec as P

HALF = 4
GROUPS = 2
TAP_ROWS = 96
MESH = pl.DeviceIdType.MESH
BF16 = jnp.bfloat16
F32 = jnp.float32


def halves(table):
    high = table.astype(np.float32).astype(ml_dtypes.bfloat16)
    low = (table - high.astype(np.float64)).astype(np.float32).astype(ml_dtypes.bfloat16)
    return np.stack((high, low))


def bin_groups(frequencies):
    order = np.concatenate((np.arange(0, frequencies, 2), np.arange(1, frequencies, 2)))
    return order.reshape(GROUPS, frequencies // GROUPS)


def temporal_tables(samples, frequencies):
    time = np.arange(samples // 2)[:, None]
    forward, inverse = [], []
    for bins in bin_groups(frequencies):
        angle = 2.0 * np.pi * (time * bins[None, :] % samples) / samples
        weight = np.where(bins == 0, 1.0, 2.0)[None, :] / samples
        forward.append(np.concatenate((np.cos(angle), -np.sin(angle)), axis=1))
        inverse.append(np.concatenate((weight * np.cos(angle), -weight * np.sin(angle)), axis=1).T)
    return halves(np.stack(forward)), halves(np.stack(inverse))


def spatial_frequencies(height, width):
    chosen = []
    for row in range(height):
        for col in range(width):
            mirror = ((height - row) % height, (width - col) % width)
            if (row, col) <= mirror:
                chosen.append((row, col, 1.0 if (row, col) == mirror else 2.0))
    return np.array(chosen)


def spatial_basis(waves, padded, height, width, positions):
    positions = np.asarray(positions)
    turns = np.outer(waves[:, 0], positions[:, 0]) / height + np.outer(waves[:, 1], positions[:, 1]) / width
    angle = 2.0 * np.pi * turns
    basis = np.zeros((2 * padded, len(positions)))
    basis[: len(waves)] = np.cos(angle)
    basis[padded : padded + len(waves)] = np.sin(angle)
    return basis


def grid(rows, cols):
    return [(row, col) for row in rows for col in cols]


def stacked(table):
    both = halves(table)
    return np.concatenate((both[0], both[1]), axis=0)


def thrice(table):
    both = halves(table)
    return np.concatenate((both[0], both[0], both[1]), axis=1)


def layout(rows, cols, sides):
    strip, ends, middle = rows * HALF, HALF * HALF, HALF * (cols - 2 * HALF)
    sizes = [("left", strip), ("right", strip)]
    for side in range(sides):
        sizes += [(("low", side), ends), (("high", side), ends), (("middle", side), middle)]
        sizes += [(("from_left", side), ends), (("from_right", side), ends)]
    places, at = {}, 0
    for name, size in sizes:
        places[name] = (at, size)
        at += size
    return places, at


def early_count(rows, sides):
    return 2 * rows * HALF + (2 * HALF * HALF if sides == 1 else 0)


def spatial_tables(rows, cols, inline_count):
    height, width = rows + 2 * HALF, cols + 2 * HALF
    waves = spatial_frequencies(height, width)
    padded = -(-len(waves) // 16) * 16
    basis = functools.partial(spatial_basis, waves, padded, height, width)
    below_zero, above_end = range(-HALF, 0), range(cols, cols + HALF)
    own = grid(range(rows), range(cols))
    above, below = range(-HALF, 0), range(rows, rows + HALF)
    variants = [[below], [above]] if inline_count == 2 else [[above, below]]
    sides = min(inline_count - 1, 2)
    second = []
    for bands in variants:
        places = grid(range(rows), below_zero) + grid(range(rows), above_end)
        for band in bands[:sides]:
            places += grid(band, range(HALF)) + grid(band, range(cols - HALF, cols))
            places += grid(band, range(HALF, cols - HALF))
            places += grid(band, below_zero) + grid(band, above_end)
        soon = early_count(rows, sides)
        early, late = thrice(basis(places[:soon])), thrice(basis(places[soon:]))
        early = np.pad(early, ((0, 0), (0, -early.shape[1] % 128)))
        second.append(np.concatenate((early, late), axis=1))
    reach = range(-HALF, HALF + 1)
    taps = np.zeros((2 * padded, TAP_ROWS))
    taps[:, : len(reach) ** 2] = basis(grid(reach, reach))
    count = np.zeros((2 * padded, 1))
    count[: len(waves), 0] = waves[:, 2] / (height * width)
    count[padded : padded + len(waves), 0] = -waves[:, 2] / (height * width)
    back = (count * basis(own)).T
    return thrice(basis(own)), np.stack(second), thrice(taps), stacked(back)


def parts(value):
    high = value.astype(BF16)
    return high, (value - high.astype(F32)).astype(BF16)


def product(left, high, low):
    dot = functools.partial(jnp.dot, preferred_element_type=F32)
    count = left.shape[0] // 2
    both = dot(left, high)
    return both[:count] + (both[count:] + dot(left[:count], low))


def summed(left, high, low):
    return jnp.dot(left, jnp.concatenate((high, low, high), axis=0), preferred_element_type=F32)


def kernel(
    rows, cols, inline_count, xline_count,
    traces, filters, temporal, spatial,
    out,
    own_in, own, own_high, own_low, ends, middle, halo, wave, response, kept, tap_rows,
    filters_in, forward_in, inverse_in, first_in, second_in, taps_in, back_in, order_in,
    local_sem, send_sem, recv_sem,
):
    sides = min(inline_count - 1, 2)
    places, _ = layout(rows, cols, sides)
    fold = own_in.shape[1] // 2
    lanes = wave.shape[2]
    bins = lanes // 2
    padded = wave.shape[1] // 2
    inner = cols - 2 * HALF

    me_i = lax.axis_index("inline")
    me_x = lax.axis_index("xline")

    has_left, has_right = me_x > 0, me_x < xline_count - 1
    at_left, at_right = {"xline": me_x - 1}, {"xline": me_x + 1}
    if inline_count == 2:
        bands = [(None, {"inline": 1 - me_i}, (1 - me_i) * (rows - HALF), 0)]
        present = [None]
    elif inline_count > 2:
        has_above, has_below = me_i > 0, me_i < inline_count - 1
        bands = [
            (has_above, {"inline": me_i - 1}, 0, 1),
            (has_below, {"inline": me_i + 1}, rows - HALF, 0),
        ]
        present = [has_above, has_below]
    else:
        bands, present = [], []

    def when(condition, action):
        if condition is None:
            action()
        else:
            pl.when(condition)(action)

    barrier = pltpu.get_barrier_semaphore()
    neighbours = [(has_left, at_left), (has_right, at_right)]
    neighbours += [(exists, where) for exists, where, _, _ in bands]
    for exists, where in neighbours:
        when(exists, lambda: pl.semaphore_signal(barrier, inc=1, device_id=where, device_id_type=MESH))

    def load(source, target, slot):
        return pltpu.make_async_copy(source, target, local_sem.at[slot])

    load_own = load(traces, own_in, 0)
    load_forward = [load(temporal.at[0, :, group], forward_in.at[:, group], 1 + group) for group in range(GROUPS)]
    waves = wave.shape[1]

    def table(start, target, slot):
        count = target.shape[0]
        return load(spatial.at[pl.ds(start, count)], target, slot)

    base = 1 + GROUPS
    load_filters = load(filters, filters_in, base)
    frequencies = order_in.shape[0]
    load_order = table(0, order_in, base + 1)
    load_taps = table(frequencies, taps_in, base + 2)
    load_first = table(frequencies + waves, first_in, base + 3)
    after = frequencies + 2 * waves
    load_back = table(after, back_in, base + 5)
    after += back_in.shape[0]
    if inline_count == 2:
        after = pl.multiple_of(after + me_i * waves, 16)
    load_second = table(after, second_in, base + 4)
    load_inverse = load(temporal.at[1], inverse_in, base + 6)
    loads = [load_own, *load_forward, load_filters, load_order, load_taps]
    loads += [load_first, load_second, load_back, load_inverse]
    for each in loads:
        each.start()

    def clear(*names):
        for name in names:
            at, size = places[name]
            halo[:, at : at + size, :] = jnp.zeros((GROUPS, size, lanes), F32)

    pl.when(jnp.logical_not(has_left))(lambda: clear("left", *[("from_left", s) for s in range(sides)]))
    pl.when(jnp.logical_not(has_right))(lambda: clear("right", *[("from_right", s) for s in range(sides)]))
    for side, exists in enumerate(present):
        if exists is not None:
            pieces = [(kind, side) for kind in ("low", "high", "middle", "from_left", "from_right")]
            pl.when(jnp.logical_not(exists))(lambda: clear(*pieces))

    slots = {name: slot for slot, name in enumerate(places)}

    def remote(group, name, source, where):
        at, size = places[name]
        slot = group * len(places) + slots[name]
        return pltpu.make_async_remote_copy(
            src_ref=source,
            dst_ref=halo.at[group, pl.ds(at, size)],
            send_sem=send_sem.at[slot],
            recv_sem=recv_sem.at[slot],
            device_id=where,
            device_id_type=MESH,
        )

    def landed(group, name):
        at, size = places[name]
        return halo.at[group, pl.ds(at, size)]

    def come(group, name):
        remote(group, name, landed(group, name), at_left).wait_recv()

    sent = []

    def send(condition, copy):
        when(condition, copy.start)
        sent.append((condition, copy))

    load_own.wait()
    for group in range(GROUPS):
        if group % (GROUPS // 2) == 0:
            if group == 0:
                folded = own_in[:, :fold] + own_in[:, fold:]
            else:
                folded = own_in[:, :fold] - own_in[:, fold:]
            folded = jnp.concatenate(parts(folded), axis=0)
        load_forward[group].wait()
        spectrum = product(folded, forward_in[0, group], forward_in[1, group])
        own[...] = spectrum
        high, low = parts(spectrum)
        own_high[group] = high
        own_low[group] = low
        for row in range(rows):
            at = row * cols
            ends[group, 0, row * HALF : (row + 1) * HALF, :] = own[at : at + HALF, :]
            ends[group, 1, row * HALF : (row + 1) * HALF, :] = own[at + cols - HALF : at + cols, :]
            middle[group, row * inner : (row + 1) * inner, :] = own[at + HALF : at + cols - HALF, :]
        if group == 0:
            peers = sum(1 if exists is None else exists.astype(jnp.int32) for exists, _ in neighbours)
            pl.semaphore_wait(barrier, peers)
        for exists, where, start, side in bands:
            few = pl.ds(pl.multiple_of(start * HALF, HALF * HALF), HALF * HALF)
            send(exists, remote(group, ("low", side), ends.at[group, 0, few], where))
            send(exists, remote(group, ("high", side), ends.at[group, 1, few], where))
        send(has_left, remote(group, "right", ends.at[group, 0], at_left))
        send(has_right, remote(group, "left", ends.at[group, 1], at_right))
    for group in range(GROUPS):
        for exists, where, start, side in bands:
            many = pl.ds(pl.multiple_of(start * inner, HALF * inner), HALF * inner)
            send(exists, remote(group, ("middle", side), middle.at[group, many], where))

    def forward_ends(group):
        for side, exists in enumerate(present):
            def on(side=side):
                come(group, ("low", side))
                come(group, ("high", side))
                to_left = remote(group, ("from_right", side), landed(group, ("low", side)), at_left)
                to_right = remote(group, ("from_left", side), landed(group, ("high", side)), at_right)
                pl.when(has_left)(to_left.start)
                pl.when(has_right)(to_right.start)

            when(exists, on)

    def sent_ends(group):
        for side, exists in enumerate(present):
            def on(side=side):
                to_left = remote(group, ("from_right", side), landed(group, ("low", side)), at_left)
                to_right = remote(group, ("from_left", side), landed(group, ("high", side)), at_right)
                pl.when(has_left)(to_left.wait_send)
                pl.when(has_right)(to_right.wait_send)

            when(exists, on)

    forward_ends(0)
    load_filters.wait()
    load_order.wait()
    load_taps.wait()
    tap_count = filters_in.shape[0]
    tap_rows[...] = jnp.zeros_like(tap_rows)
    for part in range(2):
        tap_rows[part, :tap_count, :] = filters_in[:, part, :]
    real, imag = parts(tap_rows[0]), parts(tap_rows[1])
    ordered = jnp.dot(
        jnp.concatenate((real[0], imag[0], real[1], imag[1]), axis=0),
        order_in[:, :frequencies],
        preferred_element_type=F32
    ).astype(BF16)
    for group in range(GROUPS):
        mine = slice(group * bins, (group + 1) * bins)
        pieces = [ordered[TAP_ROWS * piece : TAP_ROWS * (piece + 1), mine] for piece in range(4)]
        response[group] = summed(
            taps_in[:, : 3 * TAP_ROWS], jnp.concatenate(pieces[:2], axis=1), jnp.concatenate(pieces[2:], axis=1)
        )
        if group < GROUPS - 1:
            forward_ends(group + 1)
    load_first.wait()
    load_second.wait()
    soon = early_count(rows, sides)
    late_at = -(-3 * soon // 128) * 128
    late = halo.shape[1] - soon
    for group in range(GROUPS):
        wave[group] = summed(first_in[:, : 3 * rows * cols], own_high[group], own_low[group])
    for group in range(GROUPS):
        pl.when(has_left)(lambda: come(group, "left"))
        pl.when(has_right)(lambda: come(group, "right"))
        high, low = parts(halo[group, :soon])
        wave[group] += summed(second_in[:, : 3 * soon], high, low)

    load_back.wait()
    load_inverse.wait()
    halfway = [None, None]
    for group in range(GROUPS):
        for side, exists in enumerate(present):
            def rest(side=side):
                come(group, ("middle", side))
                pl.when(has_left)(lambda: come(group, ("from_left", side)))
                pl.when(has_right)(lambda: come(group, ("from_right", side)))

            when(exists, rest)
        if late:
            high, low = parts(halo[group, soon:])
            wave[group] += summed(second_in[:, late_at : late_at + 3 * late], high, low)

        rc, rs = wave[group, :padded, :bins], wave[group, padded:, :bins]
        ic, js = wave[group, :padded, bins:], wave[group, padded:, bins:]
        frc, frs = response[group, :padded, :bins], response[group, padded:, :bins]
        fic, fis = response[group, :padded, bins:], response[group, padded:, bins:]
        outcome = {
            (0, 0): rc * frc + rs * frs - (ic * fic + js * fis),
            (1, 0): rc * frs - rs * frc - (ic * fis - js * fic),
            (0, 1): rc * fic + rs * fis + (ic * frc + js * frs),
            (1, 1): rc * fis - rs * fic + (ic * frs - js * frc),
        }
        for (which, part), value in outcome.items():
            high, low = parts(value)
            kept[0, which * padded : (which + 1) * padded, part * bins : (part + 1) * bins] = high
            kept[1, which * padded : (which + 1) * padded, part * bins : (part + 1) * bins] = low
        filtered = product(back_in[:, : 2 * padded], kept[0], kept[1])
        filtered = jnp.concatenate(parts(filtered), axis=0)
        piece = product(filtered, inverse_in[0, group], inverse_in[1, group])
        parity = group // (GROUPS // 2)
        halfway[parity] = piece if halfway[parity] is None else halfway[parity] + piece
    out[:, :fold] = halfway[0] + halfway[1]
    out[:, fold:] = halfway[0] - halfway[1]

    for condition, copy in sent:
        when(condition, copy.wait_send)
    for group in range(GROUPS):
        sent_ends(group)


def per_device(traces, filters, inline_count, xline_count):
    rows, cols, samples = traces.shape
    _, frequencies, tap_count = filters.shape
    forward, inverse = temporal_tables(samples, frequencies)
    first, second, taps, back = spatial_tables(rows, cols, inline_count)
    order = np.zeros((frequencies, frequencies), ml_dtypes.bfloat16)
    order[bin_groups(frequencies).reshape(-1), np.arange(frequencies)] = 1.0
    sides = min(inline_count - 1, 2)
    places, around = layout(rows, cols, sides)
    own = rows * cols
    waves = first.shape[0]
    lanes = 2 * frequencies // GROUPS
    pieces = [order, taps, first, back, *second]
    wide = -(-max(piece.shape[1] for piece in pieces) // 128) * 128
    spatial = np.concatenate([np.pad(piece, ((0, 0), (0, wide - piece.shape[1]))) for piece in pieces])
    operands = [traces.reshape(own, samples), filters.transpose(2, 0, 1)]
    operands += [jnp.asarray(np.stack((forward, inverse))), jnp.asarray(spatial)]
    copies = GROUPS * len(places)
    result = pl.pallas_call(
        functools.partial(kernel, rows, cols, inline_count, xline_count),
        out_shape=jax.ShapeDtypeStruct((own, samples), F32),
        in_specs=[pl.BlockSpec(memory_space=pltpu.HBM)] * len(operands),
        out_specs=pl.BlockSpec(memory_space=pltpu.VMEM),
        scratch_shapes=[
            pltpu.VMEM((own, samples), F32),
            pltpu.VMEM((own, lanes), F32),
            pltpu.VMEM((GROUPS, own, lanes), BF16),
            pltpu.VMEM((GROUPS, own, lanes), BF16),
            pltpu.VMEM((GROUPS, 2, rows * HALF, lanes), F32),
            pltpu.VMEM((GROUPS, rows * (cols - 2 * HALF), lanes), F32),
            pltpu.VMEM((GROUPS, around, lanes), F32),
            pltpu.VMEM((GROUPS, waves, lanes), F32),
            pltpu.VMEM((GROUPS, waves, lanes), F32),
            pltpu.VMEM((2, waves, lanes), BF16),
            pltpu.VMEM((2, TAP_ROWS, frequencies), F32),
            pltpu.VMEM((tap_count, 2, frequencies), F32),
            pltpu.VMEM(forward.shape, BF16),
            pltpu.VMEM(inverse.shape, BF16),
            pltpu.VMEM((waves, wide), BF16),
            pltpu.VMEM((waves, wide), BF16),
            pltpu.VMEM((waves, wide), BF16),
            pltpu.VMEM((back.shape[0], wide), BF16),
            pltpu.VMEM((frequencies, wide), BF16),
            pltpu.SemaphoreType.DMA((8 + GROUPS,)),
            pltpu.SemaphoreType.DMA((copies,)),
            pltpu.SemaphoreType.DMA((copies,)),
        ],
        compiler_params=pltpu.CompilerParams(
            collective_id=0, has_side_effects=True, vmem_limit_bytes=53 * 1024 * 1024
        ),
    )(*operands)
    return result.reshape(rows, cols, samples)


def solution(mesh):
    return jax.shard_map(
        functools.partial(
            per_device, inline_count=mesh.shape["inline"], xline_count=mesh.shape["xline"]
        ),
        mesh=mesh,
        in_specs=(P("inline", "xline", None), P()),
        out_specs=P("inline", "xline", None),
        check_vma=False,
    )
```
